32 devices in a mesh: groups: 2 (over y), neg: 4 (over z), rep: 2 (over x), sub: 2 (over core).
Axes of the slice: x: 2, y: 2, z: 4, core: 2. Of those that a mesh axis runs over, the one named last changes fastest.
Arguments:
- query_feats: bfloat16 [16384, 512], P(('groups', 'neg', 'rep', 'sub')), parts along dimension 0, may hold values from -6 to 6
- item_feats: bfloat16 [8192, 512], P(('groups', 'neg', 'rep', 'sub')), parts along dimension 0, may hold values from -6 to 6
- query_proj: bfloat16 [512, 128], replicated, may hold values from -0.25 to 0.25
- item_proj: bfloat16 [512, 128], replicated, may hold values from -0.25 to 0.25
- item_ids: int32 [8192], P(('groups', 'neg', 'rep', 'sub')), parts along dimension 0, may hold values from 0 to 999999
- item_counts: int32 [8192], P(('groups', 'neg', 'rep', 'sub')), parts along dimension 0, may hold values from 1 to 999
- positives: int32 [16384], P(('groups', 'neg', 'rep', 'sub')), parts along dimension 0, may hold values from 0 to 255
Outputs:
- grad_query_proj: float32 [1024, 128], P('groups'), parts along dimension 0
- grad_item_proj: float32 [1024, 128], P('groups'), parts along dimension 0
- losses: float32 [16384], P(('groups', 'neg', 'rep', 'sub')), parts along dimension 0
The draws below stay inside these ranges and needn't reach their ends.
There are 2 independent parts, one for each index of `groups`. The reference program is written for one: setup_inputs(seed, part) draws one part's arguments, and reference() takes and returns one part's arrays. A program takes and returns all parts, laid end to end along the dimension named above; an argument that names none is the same for every part. Nothing has to cross between parts.
Inputs may be any that keep to these rules, and one draw needn't show every extreme that they name: `positives`: each value indexes one of the 256 item rows held by the query's own device.
All inputs are finite; a program needn't handle non-finite values.
Results may differ from the reference program's by a relative error of at most 0.0049.
Values may be sent and summed in bfloat16 or wider, within the bound.
No kernel may reach another device: no remote copies, remote signals or barrier semaphores. Data moves between devices by JAX's collectives and lax.ppermute only.
A program may use at most 64 MiB of HBM per device.

```python
import math
import jax
import jax.numpy as jnp
import numpy as np
from jax import lax

E = 128
DH = 512
ID_SPACE = 1000000
Q_DEV = 512
ITEMS_DEV = 256
QUERIES = 8192
ITEMS = 4096
N_NEG = 4
N_REP = 2
N_SUB = 2


def set_ends(values, rng, least, largest):
    shape = values.shape
    spot = [jax.random.randint(jax.random.fold_in(rng, axis), (), 0, shape[axis]) for axis in range(len(shape))]
    values = values.at[tuple(spot)].set(least)
    longest = shape.index(max(shape))
    spot[longest] = (spot[longest] + 1) % shape[longest]
    return values.at[tuple(spot)].set(largest)


def steps_of(key, shape, pieces, smallest, largest):
    def one(position, parts):
        heights = jax.random.uniform(jax.random.fold_in(jax.random.fold_in(key, 6), position), (parts,), jnp.float32, smallest / len(pieces), largest / len(pieces))
        return jnp.repeat(jnp.exp(heights), shape[position] // parts).reshape((-1,) + (1,) * (len(shape) - position - 1))

    gain = one(*pieces[0])
    for cut in pieces[1:]:
        gain = gain * one(*cut)
    return gain


def skewed_wide(own_key, extent, number_of, slope):
    loads = [min(1 << octave, number_of + 1 - (1 << octave)) * (1 << 20) // math.isqrt((1 << octave) ** slope) + 1 for octave in range((number_of + 1).bit_length()) if 1 << octave <= number_of]
    spread = 1 + sum(loads) // (1 << 30)
    table = np.cumsum(np.array([max(1, weight // spread) for weight in loads]))
    lot = jax.random.randint(jax.random.fold_in(own_key, 1), extent, 0, int(table[len(loads) - 1]))
    start = jnp.left_shift(1, jnp.searchsorted(jnp.asarray(table, jnp.int32), lot, side="right").astype(jnp.int32))
    standing = start - 1 + jax.random.randint(jax.random.fold_in(own_key, 4), extent, 0, 1 << 30) % jnp.minimum(start, number_of + 1 - start)
    return jax.random.permutation(jax.random.fold_in(own_key, 2), number_of)[standing].astype(jnp.int32)


def bell_draw(key, extent, spread, most, shards=(), held_as=jnp.bfloat16):
    factor_of = steps_of(key, extent, shards, -0.22, 0.18) if shards else 1.0
    values = jax.random.normal(key, extent, jnp.float32) * spread * factor_of
    return jnp.minimum(jnp.maximum(values, -most), most).astype(held_as)


def setup_inputs(seed: int = 0, part: int = 0) -> dict:
    key_of = jax.random.split(jax.random.key(seed), 8)
    part_splits = jax.random.split(jax.random.fold_in(key_of[7], part), 8)
    return {
        "query_feats": bell_draw(part_splits[0], (QUERIES, DH), 1.0, 6.0, ((0, 16),)),
        "item_feats": bell_draw(part_splits[1], (ITEMS, DH), 1.0, 6.0, ((0, 16),)),
        "query_proj": bell_draw(key_of[2], (DH, E), DH ** -0.5, 0.25),
        "item_proj": bell_draw(key_of[3], (DH, E), DH ** -0.5, 0.25),
        "item_ids": set_ends(skewed_wide(part_splits[4], (ITEMS,), ID_SPACE, 2), jax.random.fold_in(part_splits[4], 3), 0, ID_SPACE - 1).astype(jnp.int32),
        "item_counts": set_ends(jax.random.randint(part_splits[5], (ITEMS,), 1, 1000), jax.random.fold_in(part_splits[5], 1), 1, 999).astype(jnp.int32),
        "positives": set_ends(jax.random.randint(part_splits[6], (QUERIES,), 0, ITEMS_DEV), jax.random.fold_in(part_splits[6], 1), 0, ITEMS_DEV - 1).astype(jnp.int32),
    }


inverse_softness = 20.0

def normalize(values):
    return values / jnp.sqrt(lax.optimization_barrier(jnp.sum(values * values, axis=-1, keepdims=True)) + 1e-06)

def reference(query_feats, item_feats, query_proj, item_proj, item_ids, item_counts, positives):
    n_neg = N_NEG
    n_cols = N_REP * N_SUB
    request_number = Q_DEV
    i_rows = ITEMS_DEV
    width = E
    adjusted_derivative = inverse_softness / request_number
    query_z = jnp.dot(query_feats.astype(jnp.float32), query_proj.astype(jnp.float32))
    item_z = jnp.dot(item_feats.astype(jnp.float32), item_proj.astype(jnp.float32))
    query_batch = normalize(query_z).astype(jnp.bfloat16)
    items = normalize(item_z).astype(jnp.bfloat16)
    logq = jnp.log(item_counts.astype(jnp.float32))
    query_grid = query_batch.reshape(n_neg, n_cols, request_number, width).transpose(1, 0, 2, 3)
    item_grid = items.reshape(n_neg, n_cols, i_rows, width).transpose(1, 0, 2, 3)
    logq_grid = logq.reshape(n_neg, n_cols, i_rows).transpose(1, 0, 2)
    ids_grid = item_ids.reshape(n_neg, n_cols, i_rows).transpose(1, 0, 2)
    pos_grid = positives.reshape(n_neg, n_cols, request_number).transpose(1, 0, 2)
    pos_id_grid = jnp.take_along_axis(ids_grid, pos_grid, axis=2)

    def column(inputs):
        query_col, item_col, logq_col, ids_col, pos_col, pos_id_col = inputs
        catalog_entry_list = item_col.reshape(n_neg * i_rows, width).astype(jnp.float32)
        drawn_proposal_logdensity = logq_col.reshape(n_neg * i_rows)
        flat_ids = ids_col.reshape(n_neg * i_rows)
        cand_index = jnp.arange(n_neg * i_rows).astype(jnp.int32)

        def step(item_acc, xs):
            index, query_block, pos_block, pos_id_block = xs
            request_vectors_wide = query_block.astype(jnp.float32)
            similarity_table = inverse_softness * jnp.dot(request_vectors_wide, catalog_entry_list.T) - drawn_proposal_logdensity[None, :]
            pos_global = (index * i_rows + pos_block).astype(jnp.int32)
            onehot = cand_index[None, :] == pos_global[:, None]
            collide = (flat_ids[None, :] == pos_id_block[:, None]) & jnp.logical_not(onehot)
            weights = jnp.where(collide, jnp.float32(0.0), jnp.exp(similarity_table))
            totals = lax.optimization_barrier(jnp.sum(weights, axis=1))
            target_similarity = jnp.take_along_axis(similarity_table, pos_global[:, None], axis=1)[:, 0]
            loss_block = jnp.log(totals) - target_similarity
            weights_b = lax.optimization_barrier(weights.astype(jnp.bfloat16)).astype(jnp.float32)
            weighted = jnp.dot(weights_b, catalog_entry_list)
            pos_items = jnp.take(catalog_entry_list, pos_global, axis=0)
            query_cot = (weighted / totals[:, None] - pos_items) * adjusted_derivative
            grads = (weights / totals[:, None] - onehot.astype(jnp.float32)).astype(jnp.bfloat16)
            grads_f = grads.astype(jnp.float32)
            item_acc = item_acc + jnp.dot(grads_f.T, request_vectors_wide)
            return (item_acc, (loss_block, query_cot))
        start_acc = jnp.zeros((n_neg * i_rows, width), jnp.float32)
        item_acc, (loss_col, query_cot_col) = lax.scan(step, start_acc, (jnp.arange(n_neg).astype(jnp.int32), query_col, pos_col, pos_id_col))
        return (loss_col, query_cot_col, (item_acc * adjusted_derivative).reshape(n_neg, i_rows, width))
    loss_all, query_cot, item_cot = lax.map(column, (query_grid, item_grid, logq_grid, ids_grid, pos_grid, pos_id_grid))
    losses = loss_all.transpose(1, 0, 2).reshape(-1)
    query_cot = query_cot.transpose(1, 0, 2, 3).reshape(-1, width)
    item_cot = item_cot.transpose(1, 0, 2, 3).reshape(-1, width)
    query_dz = jax.vjp(normalize, query_z)[1](query_cot)[0].astype(jnp.bfloat16)
    item_dz = jax.vjp(normalize, item_z)[1](item_cot)[0].astype(jnp.bfloat16)
    grad_query_proj = jnp.dot(query_feats.astype(jnp.float32).T, query_dz.astype(jnp.float32))
    grad_item_proj = jnp.dot(item_feats.astype(jnp.float32).T, item_dz.astype(jnp.float32))
    return (grad_query_proj, grad_item_proj, losses)
```

```python
import functools
import math

import jax
import jax.numpy as jnp
from jax import lax
from jax.experimental import pallas as pl
from jax.experimental.pallas import tpu as pltpu
from jax.sharding import PartitionSpec as P

inverse_softness = 20.0
epsilon = 1e-06
log2e = math.log2(math.e)
ln2 = math.log(2.0)
tail_rows = 16
f32 = jnp.float32
bf16 = jnp.bfloat16


def contract(lhs, rhs, over):
    return lax.dot_general(lhs, rhs, (((over[0],), (over[1],)), ((), ())), preferred_element_type=f32)


def split_terms(values):
    terms = []
    for _ in range(3):
        term = values.astype(bf16).astype(f32)
        terms.append(term)
        values = values - term
    return terms


def item_tower(feats_ref, proj_ref, ids_ref, counts_ref, message_ref, z_ref):
    rows = feats_ref.shape[0]
    z = jnp.dot(feats_ref[...], proj_ref[...], preferred_element_type=f32)
    z_ref[...] = z
    inverse = 1.0 / jnp.sqrt(jnp.sum(z * z, axis=1, keepdims=True) + epsilon)
    message_ref[0:rows, :] = (z * inverse).astype(bf16)
    ids = ids_ref[...]
    digits = [ids >> 16, (ids >> 8) & 255, ids & 255]
    log_counts = jnp.log(counts_ref[...].astype(f32)) * log2e
    lines = [digit.astype(f32) for digit in digits] + split_terms(log_counts)
    halves = ids.shape[0]
    lines.append(jnp.zeros((tail_rows - 6 * halves, ids.shape[1]), f32))
    message_ref[rows : rows + tail_rows, :] = jnp.concatenate(lines, axis=0).astype(bf16)


def item_columns(message_ref, half, halves):
    rows = message_ref.shape[0] - tail_rows
    tail = message_ref[rows : rows + tail_rows, :]
    line = lax.broadcasted_iota(jnp.int32, (tail_rows, 128), 0)

    def weights(scales, first):
        table = jnp.zeros((tail_rows, 128), f32)
        for step, scale in enumerate(scales):
            table = jnp.where(line == (first + step) * halves + half, scale, table)
        return table.astype(bf16)

    ids = contract(tail, weights((65536.0, 256.0, 1.0), 0), (0, 0))
    logs = contract(tail, weights((1.0, 1.0, 1.0), 3), (0, 0))
    return ids, logs


def wide(column, width):
    return jnp.concatenate([column] * (width // column.shape[1]), axis=1)


def query_tower(
    feats_ref, proj_ref, message_ref, positives_ref, z_ref, query_ref, weights_ref, weighted_ref, pos_ref, lines_ref
):
    rows = message_ref.shape[0] - tail_rows
    halves = rows // 128
    z = contract(proj_ref[...], feats_ref[...], (0, 1))
    z_ref[...] = z
    inverse = 1.0 / jnp.sqrt(jnp.sum(z * z, axis=0, keepdims=True) + epsilon)
    queries = (z * inverse).astype(bf16)
    query_ref[...] = queries
    count = queries.shape[1]
    positives = positives_ref[...]
    tail = message_ref[rows : rows + tail_rows, :]
    own = []
    pos_id = jnp.zeros((1, count), f32)
    for half in range(halves):
        spot = lax.broadcasted_iota(jnp.int32, (128, count), 0) + half * 128
        own.append(spot == positives)
        found = jnp.dot(tail, own[half].astype(f32).astype(bf16), preferred_element_type=f32)
        for step, scale in enumerate((65536.0, 256.0, 1.0)):
            line = step * halves + half
            pos_id = pos_id + scale * found[line : line + 1, :]
    totals = jnp.zeros((1, count), f32)
    target = jnp.zeros((1, count), f32)
    weighted = jnp.zeros((queries.shape[0], count), f32)
    pos_items = jnp.zeros((queries.shape[0], count), f32)
    for half in range(halves):
        items = message_ref[half * 128 : half * 128 + 128, :]
        ids, logs = item_columns(message_ref, half, halves)
        scores = jnp.dot(items, queries, preferred_element_type=f32)
        scores = scores * (inverse_softness * log2e) - wide(logs, count)
        collide = (wide(ids, count) == pos_id) & jnp.logical_not(own[half])
        weights = jnp.where(collide, 0.0, jnp.exp2(scores))
        weights_ref[half * 128 : half * 128 + 128, :] = weights
        totals = totals + jnp.sum(weights, axis=0, keepdims=True)
        target = target + jnp.sum(jnp.where(own[half], scores, 0.0), axis=0, keepdims=True)
        weighted = weighted + contract(items, weights.astype(bf16), (0, 0))
        pos_items = pos_items + contract(items, own[half].astype(f32).astype(bf16), (0, 0))
    weighted_ref[...] = weighted
    pos_ref[...] = pos_items
    lines_ref[...] = jnp.concatenate([totals, target * ln2, pos_id, jnp.zeros((5, count), f32)], axis=0)


def candidates_kernel(others, query_ref, weights_ref, part_ref, lines_ref, positives_ref, *refs):
    message_refs = refs[:others]
    piece_refs = refs[others : 2 * others]
    own_ref, weighted_ref, sums_ref, losses_ref, scratch_ref = refs[2 * others :]
    rows = weights_ref.shape[0]
    halves = rows // 128
    queries = query_ref[...]
    count = queries.shape[1]
    totals = lines_ref[0:1, :]
    pos_id = lines_ref[2:3, :]
    weighted = part_ref[...]
    for other, message_ref in enumerate(message_refs):
        for half in range(halves):
            items = message_ref[half * 128 : half * 128 + 128, :]
            ids, logs = item_columns(message_ref, half, halves)
            scores = jnp.dot(items, queries, preferred_element_type=f32)
            scores = scores * (inverse_softness * log2e) - wide(logs, count)
            weights = jnp.where(wide(ids, count) == pos_id, 0.0, jnp.exp2(scores))
            scratch_ref[other, half * 128 : half * 128 + 128, :] = weights
            totals = totals + jnp.sum(weights, axis=0, keepdims=True)
            weighted = weighted + contract(items, weights.astype(bf16), (0, 0))
    weighted_ref[...] = weighted
    sums_ref[...] = totals
    losses_ref[...] = jnp.log(totals) - lines_ref[1:2, :]
    share = 1.0 / totals
    for other in range(others):
        grads = (scratch_ref[other] * share).astype(bf16)
        piece_refs[other][...] = contract(grads, queries, (1, 1)).astype(bf16)
    own = lax.broadcasted_iota(jnp.int32, (rows, count), 0) == positives_ref[...]
    grads = (weights_ref[...] * share - own.astype(f32)).astype(bf16)
    own_ref[...] = contract(grads, queries, (1, 1))


def query_gradient(scale, weighted_ref, sums_ref, pos_ref, z_ref, feats_ref, item_feats_ref, grad_ref, turned_ref):
    cot = (weighted_ref[...] / sums_ref[...] - pos_ref[...]) * scale
    z = z_ref[...]
    inverse = 1.0 / jnp.sqrt(jnp.sum(z * z, axis=0, keepdims=True) + epsilon)
    along = jnp.sum(z * cot, axis=0, keepdims=True) * (inverse * inverse * inverse)
    dz = (cot * inverse - z * along).astype(bf16)
    grad_ref[...] = contract(feats_ref[...], dz, (0, 1))
    turned_ref[...] = item_feats_ref[...].T


def item_gradient(scale, others, sub_ref, own_ref, z_ref, turned_ref, query_grad_ref, *refs):
    keep_ref, send_ref = refs[others:]
    cot = own_ref[...]
    for ref in refs[:others]:
        cot = cot + ref[...].astype(f32)
    cot = cot * scale
    z = z_ref[...]
    inverse = 1.0 / jnp.sqrt(jnp.sum(z * z, axis=1, keepdims=True) + epsilon)
    along = jnp.sum(z * cot, axis=1, keepdims=True) * (inverse * inverse * inverse)
    dz = (cot * inverse - z * along).astype(bf16)
    grad = jnp.dot(turned_ref[...], dz, preferred_element_type=f32)
    first = sub_ref[0] == 0
    query_grad = query_grad_ref[...]
    keep_ref[...] = jnp.where(first, query_grad, grad)
    send_ref[...] = jnp.where(first, grad, query_grad)


def call(kernel, outs, args, scratch=(), scalars=0, flops=0):
    vmem = pl.BlockSpec(memory_space=pltpu.VMEM)
    smem = pl.BlockSpec(memory_space=pltpu.SMEM)
    moved = sum(math.prod(s.shape) * s.dtype.itemsize for s in list(outs) + list(args))
    return pl.pallas_call(
        kernel,
        out_shape=tuple(jax.ShapeDtypeStruct(s.shape, s.dtype) for s in outs),
        in_specs=[smem] * scalars + [vmem] * (len(args) - scalars),
        out_specs=tuple([vmem] * len(outs)),
        scratch_shapes=list(scratch),
        compiler_params=pltpu.CompilerParams(vmem_limit_bytes=32 * 1024 * 1024),
        cost_estimate=pl.CostEstimate(flops=flops, bytes_accessed=moved, transcendentals=0),
    )(*args)


def out(shape, dtype=f32):
    return jax.ShapeDtypeStruct(shape, dtype)


def partners(count):
    if count & (count - 1) == 0:
        return [[(j, j ^ step) for j in range(count)] for step in range(1, count)]
    return [[(j, (j + step) % count) for j in range(count)] for step in range(1, count)]


def sent_back(pairs):
    return [(target, source) for source, target in pairs]


def sum_over(values, axis):
    size = lax.axis_size(axis)
    if size == 1:
        return values
    if size not in (2, 4):
        return lax.psum(values, axis)
    values = values.astype(bf16)
    got = [lax.ppermute(values, axis, pairs).astype(f32) for pairs in partners(size)]
    total = values.astype(f32) + got[0]
    return total + (got[1] + got[2]) if size == 4 else total


def scatter_sum(values, axis):
    size = lax.axis_size(axis)
    me = lax.axis_index(axis)
    piece = values.shape[0] // size
    total = lax.dynamic_slice_in_dim(values, me * piece, piece, 0)
    for pairs in partners(size):
        target = jnp.asarray([t for _, t in pairs], jnp.int32)[me] if size > 2 else 1 - me
        sent = lax.dynamic_slice_in_dim(values, target * piece, piece, 0)
        total = total + lax.ppermute(sent.astype(bf16), axis, pairs).astype(f32)
    return total


def gather_pieces(values, axis):
    size = lax.axis_size(axis)
    me = lax.axis_index(axis)
    piece = values.shape[0]
    whole = jnp.zeros((size * piece,) + values.shape[1:], values.dtype)
    whole = lax.dynamic_update_slice_in_dim(whole, values, me * piece, 0)
    for pairs in partners(size):
        source = jnp.asarray([s for s, _ in sorted(pairs, key=lambda p: p[1])], jnp.int32)[me] if size > 2 else 1 - me
        whole = lax.dynamic_update_slice_in_dim(whole, lax.ppermute(values, axis, pairs), source * piece, 0)
    return whole


def on_device(query_feats, item_feats, query_proj, item_proj, item_ids, item_counts, positives):
    count, hidden = query_feats.shape
    rows = item_feats.shape[0]
    width = query_proj.shape[1]
    scale = inverse_softness / count
    halves = rows // 128
    exchange = partners(lax.axis_size("neg"))
    others = len(exchange)
    message, item_z = call(
        item_tower,
        [out((rows + tail_rows, width), bf16), out((rows, width))],
        [item_feats, item_proj, item_ids.reshape(halves, 128), item_counts.reshape(halves, 128)],
        flops=2 * rows * hidden * width,
    )
    received = [lax.ppermute(message, "neg", pairs) for pairs in exchange]
    spots = positives.reshape(1, count)
    query_z, queries, own_weights, part, pos_items, lines = call(
        query_tower,
        [
            out((width, count)),
            out((width, count), bf16),
            out((rows, count)),
            out((width, count)),
            out((width, count)),
            out((8, count)),
        ],
        [query_feats, query_proj, message, spots],
        flops=2 * count * width * (hidden + 3 * rows),
    )
    results = call(
        functools.partial(candidates_kernel, others),
        [out((rows, width), bf16)] * others + [out((rows, width)), out((width, count)), out((1, count)), out((1, count))],
        [queries, own_weights, part, lines, spots] + received,
        scratch=[pltpu.VMEM((others, rows, count), f32)],
        flops=6 * count * width * rows * (others + 1),
    )
    pieces = results[:others]
    own_piece, weighted, sums, losses = results[others:]
    back = [lax.ppermute(piece, "neg", sent_back(pairs)) for piece, pairs in zip(pieces, exchange)]
    query_grad, turned = call(
        functools.partial(query_gradient, scale),
        [out((hidden, width)), out((hidden, rows), bf16)],
        [weighted, sums, pos_items, query_z, query_feats, item_feats],
        flops=2 * count * width * hidden,
    )
    sub = lax.axis_index("sub")
    keep, send = call(
        functools.partial(item_gradient, scale, others),
        [out((hidden, width)), out((hidden, width))],
        [sub.reshape(1).astype(jnp.int32), own_piece, item_z, turned, query_grad] + back,
        scalars=1,
        flops=2 * rows * width * hidden,
    )
    swap = [(0, 1), (1, 0)]
    half = keep + lax.ppermute(send, "sub", swap)
    half = sum_over(scatter_sum(half, "rep"), "neg").astype(bf16)
    mine = gather_pieces(half, "rep")
    other = lax.ppermute(mine, "sub", swap)
    first = sub == 0
    grad_query = jnp.where(first, mine, other).astype(f32)
    grad_item = jnp.where(first, other, mine).astype(f32)
    return (grad_query, grad_item, losses.reshape(count))


def solution(mesh):
    split = ("groups", "neg", "rep", "sub")
    return jax.shard_map(
        on_device,
        mesh=mesh,
        in_specs=(P(split, None), P(split, None), P(), P(), P(split), P(split), P(split)),
        out_specs=(P("groups", None), P("groups", None), P(split)),
        check_vma=False,
    )
```

```python
import functools
import math

import jax
import jax.numpy as jnp
from jax import lax
from jax.experimental import pallas as pl
from jax.experimental.pallas import tpu as pltpu
from jax.sharding import PartitionSpec as P

inverse_softness = 20.0
epsilon = 1e-06
log2e = math.log2(math.e)
ln2 = math.log(2.0)
tail_rows = 16
f32 = jnp.float32
bf16 = jnp.bfloat16


def contract(lhs, rhs, over):
    return lax.dot_general(lhs, rhs, (((over[0],), (over[1],)), ((), ())), preferred_element_type=f32)


def split_terms(values):
    terms = []
    for _ in range(3):
        term = values.astype(bf16).astype(f32)
        terms.append(term)
        values = values - term
    return terms


def item_tower(feats_hbm, proj_hbm, ids_hbm, counts_hbm, message_ref, z_ref, feats_ref, proj_ref, ids_ref, counts_ref, sems):
    pairs = ((ids_hbm, ids_ref), (counts_hbm, counts_ref), (proj_hbm, proj_ref), (feats_hbm, feats_ref))
    copies = [pltpu.make_async_copy(source, target, sems.at[k]) for k, (source, target) in enumerate(pairs)]
    for copy in copies:
        copy.start()
    rows = feats_ref.shape[0]
    copies[0].wait()
    copies[1].wait()
    ids = ids_ref[...]
    digits = [ids >> 16, (ids >> 8) & 255, ids & 255]
    log_counts = jnp.log(counts_ref[...].astype(f32)) * log2e
    lines = [digit.astype(f32) for digit in digits] + split_terms(log_counts)
    halves = ids.shape[0]
    lines.append(jnp.zeros((tail_rows - 6 * halves, ids.shape[1]), f32))
    message_ref[rows : rows + tail_rows, :] = jnp.concatenate(lines, axis=0).astype(bf16)
    copies[2].wait()
    copies[3].wait()
    z = jnp.dot(feats_ref[...], proj_ref[...], preferred_element_type=f32)
    z_ref[...] = z
    inverse = 1.0 / jnp.sqrt(jnp.sum(z * z, axis=1, keepdims=True) + epsilon)
    message_ref[0:rows, :] = (z * inverse).astype(bf16)


def item_columns(message_ref, half, halves):
    rows = message_ref.shape[0] - tail_rows
    tail = message_ref[rows : rows + tail_rows, :]
    line = lax.broadcasted_iota(jnp.int32, (tail_rows, 128), 0)

    def weights(scales, first):
        table = jnp.zeros((tail_rows, 128), f32)
        for step, scale in enumerate(scales):
            table = jnp.where(line == (first + step) * halves + half, scale, table)
        return table.astype(bf16)

    ids = contract(tail, weights((65536.0, 256.0, 1.0), 0), (0, 0))
    logs = contract(tail, weights((1.0, 1.0, 1.0), 3), (0, 0))
    return ids, logs


def wide(column, width):
    return jnp.concatenate([column] * (width // column.shape[1]), axis=1)


def block_scores(message_ref, queries, half):
    items = message_ref[half * 128 : half * 128 + 128, :]
    ids, logs = item_columns(message_ref, half, (message_ref.shape[0] - tail_rows) // 128)
    return items, ids, logs, jnp.dot(items, queries, preferred_element_type=f32)


def query_tower(
    feats_ref,
    proj_ref,
    message_ref,
    positives_ref,
    item_feats_ref,
    z_ref,
    query_ref,
    plain_ref,
    weights_ref,
    weighted_ref,
    pos_ref,
    lines_ref,
    turned_ref,
    item_turned_ref,
):
    rows = message_ref.shape[0] - tail_rows
    halves = rows // 128
    z = contract(proj_ref[...], feats_ref[...], (0, 1))
    z_ref[...] = z
    inverse = 1.0 / jnp.sqrt(jnp.sum(z * z, axis=0, keepdims=True) + epsilon)
    scaled = z * inverse
    queries = scaled.astype(bf16)
    query_ref[...] = queries
    plain_ref[...] = queries.T
    count = queries.shape[1]
    positives = positives_ref[...]
    tail = message_ref[rows : rows + tail_rows, :]
    own = []
    pos_id = jnp.zeros((1, count), f32)
    for half in range(halves):
        spot = lax.broadcasted_iota(jnp.int32, (128, count), 0) + half * 128
        own.append(spot == positives)
        found = jnp.dot(tail, own[half].astype(f32).astype(bf16), preferred_element_type=f32)
        for step, scale in enumerate((65536.0, 256.0, 1.0)):
            line = step * halves + half
            pos_id = pos_id + scale * found[line : line + 1, :]
    totals = jnp.zeros((1, count), f32)
    target = jnp.zeros((1, count), f32)
    weighted = jnp.zeros((queries.shape[0], count), f32)
    pos_items = jnp.zeros((queries.shape[0], count), f32)
    for half in range(halves):
        items, ids, logs, scores = block_scores(message_ref, queries, half)
        scores = scores * (inverse_softness * log2e) - wide(logs, count)
        collide = (wide(ids, count) == pos_id) & jnp.logical_not(own[half])
        weights = jnp.where(collide, 0.0, jnp.exp2(scores))
        weights_ref[half * 128 : half * 128 + 128, :] = weights
        totals = totals + jnp.sum(weights, axis=0, keepdims=True)
        target = target + jnp.sum(jnp.where(own[half], scores, 0.0), axis=0, keepdims=True)
        weighted = weighted + contract(items, weights.astype(bf16), (0, 0))
        pos_items = pos_items + contract(items, own[half].astype(f32).astype(bf16), (0, 0))
    weighted_ref[...] = weighted
    pos_ref[...] = pos_items
    lines_ref[...] = jnp.concatenate([totals, target * ln2, pos_id, jnp.zeros((5, count), f32)], axis=0)
    turned_ref[...] = feats_ref[...].T
    item_turned_ref[...] = item_feats_ref[...].T


def add_block(message_ref, query_ref, lines_ref, before_ref, totals, weights_ref, chunk=32):
    queries = query_ref[...]
    count = queries.shape[1]
    pos_id = lines_ref[2:3, :]
    weighted = before_ref[...]
    partial = jnp.zeros((8, count), f32)
    for half in range(weights_ref.shape[0] // 128):
        items, ids, logs, scores = block_scores(message_ref, queries, half)
        rounded = []
        for first in range(0, 128, chunk):
            part = slice(first, first + chunk)
            exponent = scores[part] * (inverse_softness * log2e) - wide(logs[part], count)
            weights = jnp.where(wide(ids[part], count) == pos_id, 0.0, jnp.exp2(exponent))
            weights_ref[half * 128 + first : half * 128 + first + chunk, :] = weights
            for line in range(0, chunk, 8):
                partial = partial + weights[line : line + 8]
            rounded.append(weights.astype(bf16))
        weighted = weighted + contract(items, jnp.concatenate(rounded, axis=0), (0, 0))
    return totals + jnp.sum(partial, axis=0, keepdims=True), weighted


def middle_block(message_ref, query_ref, lines_ref, before_ref, totals_ref, weights_ref, after_ref, sums_ref):
    totals, weighted = add_block(message_ref, query_ref, lines_ref, before_ref, totals_ref[0:1, :], weights_ref)
    after_ref[...] = weighted
    sums_ref[...] = jnp.broadcast_to(totals, sums_ref.shape)


def last_block(scale, others, ring, *refs):
    (
        message_ref,
        query_ref,
        plain_ref,
        lines_ref,
        before_ref,
        totals_ref,
        positives_ref,
        own_weights_ref,
        pos_ref,
        z_ref,
        turned_ref,
    ) = refs[:11]
    weights_refs = refs[11 : 10 + others]
    piece_refs = refs[10 + others : 10 + 2 * others]
    own_ref, own_grad_ref, losses_ref, last_ref, grad_ref = refs[10 + 2 * others :]
    rows, count = own_weights_ref.shape
    totals, weighted = add_block(message_ref, query_ref, lines_ref, before_ref, totals_ref[0:1, :], last_ref)
    losses_ref[...] = jnp.log(totals) - lines_ref[1:2, :]
    share = 1.0 / totals
    queries = plain_ref[...]
    for piece_ref, weights_ref in zip(piece_refs, list(weights_refs) + [last_ref]):
        grads = (weights_ref[...] * share).astype(bf16)
        piece_ref[0:rows, :] = jnp.dot(grads, queries, preferred_element_type=f32).astype(bf16)
    own = lax.broadcasted_iota(jnp.int32, (rows, count), 0) == positives_ref[...]
    grads = (own_weights_ref[...] * share - own.astype(f32)).astype(bf16)
    own_ref[...] = jnp.dot(grads, queries, preferred_element_type=f32)
    cot = (weighted * share - pos_ref[...]) * scale
    z = z_ref[...]
    inverse = 1.0 / jnp.sqrt(jnp.sum(z * z, axis=0, keepdims=True) + epsilon)
    along = jnp.sum(z * cot, axis=0, keepdims=True) * (inverse * inverse * inverse)
    dz = (cot * inverse - z * along).astype(bf16)
    grad_ref[...] = contract(turned_ref[...], dz, (1, 1))
    me = lax.axis_index("neg")
    part = grad_ref.shape[0] // ring
    own_grad_ref[...] = grad_ref[pl.ds(pl.multiple_of(me * part, part), part), :]
    for step, piece_ref in enumerate(piece_refs):
        target = source_of(me, step + 1, ring)
        piece_ref[rows : rows + part, :] = grad_ref[pl.ds(pl.multiple_of(target * part, part), part), :].astype(bf16)


def item_gradient(scale, others, own_ref, own_grad_ref, z_ref, turned_ref, *refs):
    keep_ref, send_ref = refs[others:]
    rows = own_ref.shape[0]
    cot = own_ref[...]
    query_grad = own_grad_ref[...]
    for ref in refs[:others]:
        cot = cot + ref[0:rows, :].astype(f32)
        query_grad = query_grad + ref[rows:, :].astype(f32)
    cot = cot * scale
    z = z_ref[...]
    inverse = 1.0 / jnp.sqrt(jnp.sum(z * z, axis=1, keepdims=True) + epsilon)
    along = jnp.sum(z * cot, axis=1, keepdims=True) * (inverse * inverse * inverse)
    dz = (cot * inverse - z * along).astype(bf16)
    grad = jnp.dot(turned_ref[...], dz, preferred_element_type=f32)
    first = lax.axis_index("sub") == 0
    for start, whole in ((0, grad), (grad.shape[0] // 2, query_grad)):
        half = whole.shape[0] // 2
        keep_ref[start : start + half, :] = jnp.where(first, whole[:half], whole[half:])
        send_ref[start : start + half, :] = jnp.where(first, whole[half:], whole[:half])


def add_pieces(others, item_rows, own_ref, *refs):
    out_ref = refs[others]
    values = [ref[...].astype(f32) for ref in (own_ref,) + refs[:others]]
    total = values[0] + values[1]
    if others == 3:
        total = total + (values[2] + values[3])
    query_rows = own_ref.shape[0] - item_rows
    out_ref[0:item_rows, :] = total[:item_rows].astype(bf16)
    for step, value in enumerate(values):
        start = item_rows + step * query_rows
        out_ref[start : start + query_rows, :] = value[item_rows:].astype(bf16)


def final_kernel(ring, direct, mine_ref, other_ref, query_ref, item_ref):
    sub = lax.axis_index("sub")
    base = lax.axis_index("neg") if direct else 0
    half = item_ref.shape[0] // 2
    part = half // ring
    for side, ref in ((sub, mine_ref), (1 - sub, other_ref)):
        values = ref[...].astype(f32)
        item_ref[pl.ds(pl.multiple_of(side * half, half), half), :] = values[:half]
        for step in range(ring):
            source = partner_of(base, step, ring)
            start = pl.multiple_of(source * (2 * part) + side * part, part)
            query_ref[pl.ds(start, part), :] = values[half + step * part : half + (step + 1) * part]


def call(kernel, outs, args, scratch=(), flops=0, fetch=False):
    vmem = pl.BlockSpec(memory_space=pltpu.VMEM)
    moved = sum(math.prod(s.shape) * s.dtype.itemsize for s in list(outs) + list(args))
    return pl.pallas_call(
        kernel,
        out_shape=tuple(jax.ShapeDtypeStruct(s.shape, s.dtype) for s in outs),
        in_specs=[pl.BlockSpec(memory_space=pltpu.HBM) if fetch else vmem] * len(args),
        out_specs=tuple([vmem] * len(outs)),
        scratch_shapes=list(scratch),
        compiler_params=pltpu.CompilerParams(vmem_limit_bytes=32 * 1024 * 1024),
        cost_estimate=pl.CostEstimate(flops=flops, bytes_accessed=moved, transcendentals=0),
    )(*args)


def out(shape, dtype=f32):
    return jax.ShapeDtypeStruct(shape, dtype)


def partner_of(me, step, count):
    if count & (count - 1) == 0:
        return me ^ step
    return lax.rem(me + step, count)


def source_of(me, step, count):
    return partner_of(me, step if count & (count - 1) == 0 else count - step, count)


def partners(count):
    return [[(j, int(partner_of(j, step, count))) for j in range(count)] for step in range(1, count)]


def sent_back(pairs):
    return [(target, source) for source, target in pairs]


def sum_over(values, axis):
    size = lax.axis_size(axis)
    if size == 1:
        return values
    if size not in (2, 4):
        return lax.psum(values, axis)
    values = values.astype(bf16)
    got = [lax.ppermute(values, axis, pairs).astype(f32) for pairs in partners(size)]
    total = values.astype(f32) + got[0]
    return total + (got[1] + got[2]) if size == 4 else total


def on_device(query_feats, item_feats, query_proj, item_proj, item_ids, item_counts, positives):
    count, hidden = query_feats.shape
    rows = item_feats.shape[0]
    width = query_proj.shape[1]
    scale = inverse_softness / count
    halves = rows // 128
    ring = lax.axis_size("neg")
    exchange = partners(ring)
    others = len(exchange)
    part = hidden // ring
    message, item_z = call(
        item_tower,
        [out((rows + tail_rows, width), bf16), out((rows, width))],
        [item_feats, item_proj, item_ids.reshape(halves, 128), item_counts.reshape(halves, 128)],
        scratch=[
            pltpu.VMEM((rows, hidden), bf16),
            pltpu.VMEM((hidden, width), bf16),
            pltpu.VMEM((halves, 128), jnp.int32),
            pltpu.VMEM((halves, 128), jnp.int32),
            pltpu.SemaphoreType.DMA((4,)),
        ],
        flops=2 * rows * hidden * width,
        fetch=True,
    )
    received = [lax.ppermute(message, "neg", pairs) for pairs in exchange]
    spots = positives.reshape(1, count)
    query_z, queries, plain, own_weights, weighted, pos_items, lines, turned, item_turned = call(
        query_tower,
        [
            out((width, count)),
            out((width, count), bf16),
            out((count, width), bf16),
            out((rows, count)),
            out((width, count)),
            out((width, count)),
            out((8, count)),
            out((hidden, count), bf16),
            out((hidden, rows), bf16),
        ],
        [query_feats, query_proj, message, spots, item_feats],
        flops=2 * count * width * (hidden + 3 * rows),
    )
    totals = lines
    weights = []
    for block in received[:-1]:
        block_weights, weighted, totals = call(
            middle_block,
            [out((rows, count)), out((width, count)), out((8, count))],
            [block, queries, lines, weighted, totals],
            flops=4 * count * width * rows,
        )
        weights.append(block_weights)
    results = call(
        functools.partial(last_block, scale, others, ring),
        [out((rows + part, width), bf16)] * others + [out((rows, width)), out((part, width)), out((1, count))],
        [received[-1], queries, plain, lines, weighted, totals, spots, own_weights, pos_items, query_z, turned] + weights,
        scratch=[pltpu.VMEM((rows, count), f32), pltpu.VMEM((hidden, width), f32)],
        flops=6 * count * width * rows * (others + 1),
    )
    own_piece, own_grad, losses = results[others:]
    back = [lax.ppermute(piece, "neg", sent_back(pairs)) for piece, pairs in zip(results, exchange)]
    kept = (hidden + part) // 2
    keep, send = call(
        functools.partial(item_gradient, scale, others),
        [out((kept, width)), out((kept, width))],
        [own_piece, own_grad, item_z, item_turned] + back,
        flops=2 * rows * width * hidden,
    )
    swap = [(0, 1), (1, 0)]
    half = sum_over(keep + lax.ppermute(send, "sub", swap), "rep")
    direct = ring in (2, 4)
    if direct:
        half = half.astype(bf16)
        mine = call(
            functools.partial(add_pieces, others, hidden // 2),
            [out((hidden, width), bf16)],
            [half] + [lax.ppermute(half, "neg", pairs) for pairs in exchange],
        )[0]
    else:
        item_half = lax.psum(half[: hidden // 2], "neg").astype(bf16)
        query_half = lax.all_gather(half[hidden // 2 :].astype(bf16), "neg", axis=0, tiled=True)
        mine = jnp.concatenate([item_half, query_half], axis=0)
    other = lax.ppermute(mine, "sub", swap)
    grad_query, grad_item = call(
        functools.partial(final_kernel, ring, direct),
        [out((hidden, width)), out((hidden, width))],
        [mine, other],
    )
    return (grad_query, grad_item, losses.reshape(count))


def solution(mesh):
    split = ("groups", "neg", "rep", "sub")
    return jax.shard_map(
        on_device,
        mesh=mesh,
        in_specs=(P(split, None), P(split, None), P(), P(), P(split), P(split), P(split)),
        out_specs=(P("groups", None), P("groups", None), P(split)),
        check_vma=False,
    )
```

```python
import functools
import math

import jax
import jax.numpy as jnp
from jax import lax
from jax.experimental import pallas as pl
from jax.experimental.pallas import tpu as pltpu
from jax.sharding import PartitionSpec as P

inverse_softness = 20.0
epsilon = 1e-06
log2e = math.log2(math.e)
ln2 = math.log(2.0)
tail_rows = 16
f32 = jnp.float32
bf16 = jnp.bfloat16


def contract(lhs, rhs, over):
    return lax.dot_general(lhs, rhs, (((over[0],), (over[1],)), ((), ())), preferred_element_type=f32)


def split_terms(values):
    terms = []
    for _ in range(3):
        term = values.astype(bf16).astype(f32)
        terms.append(term)
        values = values - term
    return terms


def item_tower(*refs):
    hbm, rest = refs[:7], refs[7:]
    message_ref, z_ref = rest[:2]
    targets = rest[2:5] + rest[6:8] + rest[5:6] + rest[8:9]
    sems = rest[9]
    copies = [pltpu.make_async_copy(source, target, sems.at[k]) for k, (source, target) in enumerate(zip(hbm, targets))]
    order = (5, 6, 3, 4, 0, 1, 2)
    for k in order:
        copies[k].start()
    feats_ref, proj_ref, ids_ref, counts_ref = targets[5], targets[6], targets[3], targets[4]
    rows = feats_ref.shape[0]
    copies[3].wait()
    copies[4].wait()
    ids = ids_ref[...]
    digits = [ids >> 16, (ids >> 8) & 255, ids & 255]
    log_counts = jnp.log(counts_ref[...].astype(f32)) * log2e
    lines = [digit.astype(f32) for digit in digits] + split_terms(log_counts)
    halves = ids.shape[0]
    lines.append(jnp.zeros((tail_rows - 6 * halves, ids.shape[1]), f32))
    message_ref[rows : rows + tail_rows, :] = jnp.concatenate(lines, axis=0).astype(bf16)
    copies[6].wait()
    copies[5].wait()
    z = jnp.dot(feats_ref[...], proj_ref[...], preferred_element_type=f32)
    z_ref[...] = z
    inverse = 1.0 / jnp.sqrt(jnp.sum(z * z, axis=1, keepdims=True) + epsilon)
    message_ref[0:rows, :] = (z * inverse).astype(bf16)
    for k in (0, 1, 2):
        copies[k].wait()


def item_columns(message_ref, half, halves):
    rows = message_ref.shape[0] - tail_rows
    tail = message_ref[rows : rows + tail_rows, :]
    line = lax.broadcasted_iota(jnp.int32, (tail_rows, 128), 0)

    def weights(scales, first):
        table = jnp.zeros((tail_rows, 128), f32)
        for step, scale in enumerate(scales):
            table = jnp.where(line == (first + step) * halves + half, scale, table)
        return table.astype(bf16)

    ids = contract(tail, weights((65536.0, 256.0, 1.0), 0), (0, 0))
    logs = contract(tail, weights((1.0, 1.0, 1.0), 3), (0, 0))
    return ids, logs


def wide(column, width):
    return jnp.concatenate([column] * (width // column.shape[1]), axis=1)


def block_scores(message_ref, queries, half):
    items = message_ref[half * 128 : half * 128 + 128, :]
    ids, logs = item_columns(message_ref, half, (message_ref.shape[0] - tail_rows) // 128)
    return items, ids, logs, jnp.dot(items, queries, preferred_element_type=f32)


def query_tower(
    feats_ref,
    proj_ref,
    message_ref,
    positives_ref,
    item_feats_ref,
    z_ref,
    query_ref,
    plain_ref,
    weights_ref,
    weighted_ref,
    pos_ref,
    lines_ref,
    turned_ref,
    item_turned_ref,
):
    rows = message_ref.shape[0] - tail_rows
    halves = rows // 128
    z = contract(proj_ref[...], feats_ref[...], (0, 1))
    z_ref[...] = z
    inverse = 1.0 / jnp.sqrt(jnp.sum(z * z, axis=0, keepdims=True) + epsilon)
    scaled = z * inverse
    queries = scaled.astype(bf16)
    query_ref[...] = queries
    plain_ref[...] = queries.T
    count = queries.shape[1]
    positives = positives_ref[...]
    tail = message_ref[rows : rows + tail_rows, :]
    own = []
    pos_id = jnp.zeros((1, count), f32)
    for half in range(halves):
        spot = lax.broadcasted_iota(jnp.int32, (128, count), 0) + half * 128
        own.append(spot == positives)
        found = jnp.dot(tail, own[half].astype(f32).astype(bf16), preferred_element_type=f32)
        for step, scale in enumerate((65536.0, 256.0, 1.0)):
            line = step * halves + half
            pos_id = pos_id + scale * found[line : line + 1, :]
    totals = jnp.zeros((1, count), f32)
    target = jnp.zeros((1, count), f32)
    weighted = jnp.zeros((queries.shape[0], count), f32)
    pos_items = jnp.zeros((queries.shape[0], count), f32)
    for half in range(halves):
        items, ids, logs, scores = block_scores(message_ref, queries, half)
        scores = scores * (inverse_softness * log2e) - wide(logs, count)
        collide = (wide(ids, count) == pos_id) & jnp.logical_not(own[half])
        weights = jnp.where(collide, 0.0, jnp.exp2(scores))
        weights_ref[half * 128 : half * 128 + 128, :] = weights
        totals = totals + jnp.sum(weights, axis=0, keepdims=True)
        target = target + jnp.sum(jnp.where(own[half], scores, 0.0), axis=0, keepdims=True)
        weighted = weighted + contract(items, weights.astype(bf16), (0, 0))
        pos_items = pos_items + contract(items, own[half].astype(f32).astype(bf16), (0, 0))
    weighted_ref[...] = weighted
    pos_ref[...] = pos_items
    lines_ref[...] = jnp.concatenate([totals, target * ln2, pos_id, jnp.zeros((5, count), f32)], axis=0)
    turned_ref[...] = feats_ref[...].T
    item_turned_ref[...] = item_feats_ref[...].T


def add_block(message_ref, query_ref, lines_ref, before_ref, totals, weights_ref, chunk=32):
    queries = query_ref[...]
    count = queries.shape[1]
    pos_id = lines_ref[2:3, :]
    weighted = before_ref[...]
    partial = jnp.zeros((8, count), f32)
    for half in range(weights_ref.shape[0] // 128):
        items, ids, logs, scores = block_scores(message_ref, queries, half)
        rounded = []
        for first in range(0, 128, chunk):
            part = slice(first, first + chunk)
            exponent = scores[part] * (inverse_softness * log2e) - wide(logs[part], count)
            weights = jnp.where(wide(ids[part], count) == pos_id, 0.0, jnp.exp2(exponent))
            weights_ref[half * 128 + first : half * 128 + first + chunk, :] = weights
            for line in range(0, chunk, 8):
                partial = partial + weights[line : line + 8]
            rounded.append(weights.astype(bf16))
        weighted = weighted + contract(items, jnp.concatenate(rounded, axis=0), (0, 0))
    return totals + jnp.sum(partial, axis=0, keepdims=True), weighted


def middle_block(message_ref, query_ref, lines_ref, before_ref, totals_ref, weights_ref, after_ref, sums_ref):
    totals, weighted = add_block(message_ref, query_ref, lines_ref, before_ref, totals_ref[0:1, :], weights_ref)
    after_ref[...] = weighted
    sums_ref[...] = jnp.broadcast_to(totals, sums_ref.shape)


def last_block(scale, others, ring, chain, *refs):
    (
        message_ref,
        query_ref,
        plain_ref,
        lines_ref,
        before_ref,
        totals_ref,
        positives_ref,
        own_weights_ref,
        pos_ref,
        z_ref,
        turned_ref,
    ) = refs[:11]
    weights_refs = refs[11 : 10 + others]
    piece_refs = refs[10 + others : 10 + 2 * others]
    own_ref, own_grad_ref, losses_ref, last_ref, grad_ref = refs[10 + 2 * others :]
    rows, count = own_weights_ref.shape
    totals, weighted = add_block(message_ref, query_ref, lines_ref, before_ref, totals_ref[0:1, :], last_ref)
    losses_ref[...] = jnp.log(totals) - lines_ref[1:2, :]
    share = 1.0 / totals
    queries = plain_ref[...]
    for step, weights_ref in zip(chain, list(weights_refs) + [last_ref]):
        piece_ref = piece_refs[step - 1]
        grads = (weights_ref[...] * share).astype(bf16)
        piece_ref[0:rows, :] = jnp.dot(grads, queries, preferred_element_type=f32).astype(bf16)
    own = lax.broadcasted_iota(jnp.int32, (rows, count), 0) == positives_ref[...]
    grads = (own_weights_ref[...] * share - own.astype(f32)).astype(bf16)
    own_ref[...] = jnp.dot(grads, queries, preferred_element_type=f32)
    cot = (weighted * share - pos_ref[...]) * scale
    z = z_ref[...]
    inverse = 1.0 / jnp.sqrt(jnp.sum(z * z, axis=0, keepdims=True) + epsilon)
    along = jnp.sum(z * cot, axis=0, keepdims=True) * (inverse * inverse * inverse)
    dz = (cot * inverse - z * along).astype(bf16)
    grad_ref[...] = contract(turned_ref[...], dz, (1, 1))
    me = lax.axis_index("neg")
    part = grad_ref.shape[0] // ring
    own_grad_ref[...] = grad_ref[pl.ds(pl.multiple_of(me * part, part), part), :]
    for step, piece_ref in enumerate(piece_refs):
        target = source_of(me, step + 1, ring)
        piece_ref[rows : rows + part, :] = grad_ref[pl.ds(pl.multiple_of(target * part, part), part), :].astype(bf16)


def item_gradient(scale, others, own_ref, own_grad_ref, z_ref, turned_ref, *refs):
    keep_ref, send_ref = refs[others:]
    rows = own_ref.shape[0]
    cot = own_ref[...]
    query_grad = own_grad_ref[...]
    for ref in refs[:others]:
        cot = cot + ref[0:rows, :].astype(f32)
        query_grad = query_grad + ref[rows:, :].astype(f32)
    cot = cot * scale
    z = z_ref[...]
    inverse = 1.0 / jnp.sqrt(jnp.sum(z * z, axis=1, keepdims=True) + epsilon)
    along = jnp.sum(z * cot, axis=1, keepdims=True) * (inverse * inverse * inverse)
    dz = (cot * inverse - z * along).astype(bf16)
    grad = jnp.dot(turned_ref[...], dz, preferred_element_type=f32)
    first = lax.axis_index("sub") == 0
    for start, whole in ((0, grad), (grad.shape[0] // 2, query_grad)):
        half = whole.shape[0] // 2
        keep_ref[start : start + half, :] = jnp.where(first, whole[:half], whole[half:])
        send_ref[start : start + half, :] = jnp.where(first, whole[half:], whole[:half])


def add_pieces(turns, item_rows, own_ref, *refs):
    out_ref = refs[-1]
    values = [own_ref[...].astype(f32)]
    for step in range(1, len(turns) + 1):
        values.append(refs[turns.index(step)][...].astype(f32))
    total = values[0] + values[1]
    if len(values) == 4:
        total = total + (values[2] + values[3])
    query_rows = own_ref.shape[0] - item_rows
    out_ref[0:item_rows, :] = total[:item_rows].astype(bf16)
    for step, value in enumerate(values):
        start = item_rows + step * query_rows
        out_ref[start : start + query_rows, :] = value[item_rows:].astype(bf16)


def final_kernel(ring, direct, mine_ref, other_ref, query_ref, item_ref):
    sub = lax.axis_index("sub")
    base = lax.axis_index("neg") if direct else 0
    half = item_ref.shape[0] // 2
    part = half // ring
    for side, ref in ((sub, mine_ref), (1 - sub, other_ref)):
        values = ref[...].astype(f32)
        item_ref[pl.ds(pl.multiple_of(side * half, half), half), :] = values[:half]
        for step in range(ring):
            source = partner_of(base, step, ring)
            start = pl.multiple_of(source * (2 * part) + side * part, part)
            query_ref[pl.ds(start, part), :] = values[half + step * part : half + (step + 1) * part]


def call(kernel, outs, args, scratch=(), flops=0, fetch=False, room=32):
    vmem = pl.BlockSpec(memory_space=pltpu.VMEM)
    moved = sum(math.prod(s.shape) * s.dtype.itemsize for s in list(outs) + list(args))
    return pl.pallas_call(
        kernel,
        out_shape=tuple(jax.ShapeDtypeStruct(s.shape, s.dtype) for s in outs),
        in_specs=[pl.BlockSpec(memory_space=pltpu.HBM) if fetch else vmem] * len(args),
        out_specs=tuple([vmem] * len(outs)),
        scratch_shapes=list(scratch),
        compiler_params=pltpu.CompilerParams(vmem_limit_bytes=room * 1024 * 1024),
        cost_estimate=pl.CostEstimate(flops=flops, bytes_accessed=moved, transcendentals=0),
    )(*args)


def pin(values):
    return pltpu.with_memory_space_constraint(values, pltpu.HBM)


def out(shape, dtype=f32):
    return jax.ShapeDtypeStruct(shape, dtype)


def partner_of(me, step, count):
    if count & (count - 1) == 0:
        return me ^ step
    return lax.rem(me + step, count)


def source_of(me, step, count):
    return partner_of(me, step if count & (count - 1) == 0 else count - step, count)


def partners(count):
    return [[(j, int(partner_of(j, step, count))) for j in range(count)] for step in range(1, count)]


def ordered(others, order):
    return list(order) if len(order) == others else list(range(1, others + 1))


def sent_back(pairs):
    return [(target, source) for source, target in pairs]


def sum_over(values, axis):
    size = lax.axis_size(axis)
    if size == 1:
        return values
    if size not in (2, 4):
        return lax.psum(values, axis)
    values = values.astype(bf16)
    got = [lax.ppermute(values, axis, pairs).astype(f32) for pairs in partners(size)]
    total = values.astype(f32) + got[0]
    return total + (got[1] + got[2]) if size == 4 else total


def on_device(query_feats, item_feats, query_proj, item_proj, item_ids, item_counts, positives):
    count, hidden = query_feats.shape
    rows = item_feats.shape[0]
    width = query_proj.shape[1]
    scale = inverse_softness / count
    halves = rows // 128
    ring = lax.axis_size("neg")
    exchange = partners(ring)
    others = len(exchange)
    part = hidden // ring
    message, item_z, query_feats, query_proj, spots, item_feats = call(
        item_tower,
        [
            out((rows + tail_rows, width), bf16),
            out((rows, width)),
            out((count, hidden), bf16),
            out((hidden, width), bf16),
            out((1, count), jnp.int32),
            out((rows, hidden), bf16),
        ],
        [
            pin(query_feats),
            pin(query_proj),
            pin(positives.reshape(1, count)),
            pin(item_ids.reshape(halves, 128)),
            pin(item_counts.reshape(halves, 128)),
            pin(item_feats),
            pin(item_proj),
        ],
        scratch=[
            pltpu.VMEM((halves, 128), jnp.int32),
            pltpu.VMEM((halves, 128), jnp.int32),
            pltpu.VMEM((hidden, width), bf16),
            pltpu.SemaphoreType.DMA((7,)),
        ],
        flops=2 * rows * hidden * width,
        fetch=True,
        room=32,
    )
    received = [lax.ppermute(message, "neg", pairs) for pairs in exchange]
    query_z, queries, plain, own_weights, weighted, pos_items, lines, turned, item_turned = call(
        query_tower,
        [
            out((width, count)),
            out((width, count), bf16),
            out((count, width), bf16),
            out((rows, count)),
            out((width, count)),
            out((width, count)),
            out((8, count)),
            out((hidden, count), bf16),
            out((hidden, rows), bf16),
        ],
        [query_feats, query_proj, message, spots, item_feats],
        flops=2 * count * width * (hidden + 3 * rows),
    )
    totals = lines
    weights = []
    chain = ordered(others, (1, 2, 3))
    for step in chain[:-1]:
        block = received[step - 1]
        block_weights, weighted, totals = call(
            middle_block,
            [out((rows, count)), out((width, count)), out((8, count))],
            [block, queries, lines, weighted, totals],
            flops=4 * count * width * rows,
        )
        weights.append(block_weights)
    results = call(
        functools.partial(last_block, scale, others, ring, chain),
        [out((rows + part, width), bf16)] * others + [out((rows, width)), out((part, width)), out((1, count))],
        [received[chain[-1] - 1], queries, plain, lines, weighted, totals, spots, own_weights, pos_items, query_z, turned] + weights,
        scratch=[pltpu.VMEM((rows, count), f32), pltpu.VMEM((hidden, width), f32)],
        flops=6 * count * width * rows * (others + 1),
    )
    own_piece, own_grad, losses = results[others:]
    back = [lax.ppermute(piece, "neg", sent_back(pairs)) for piece, pairs in zip(results, exchange)]
    kept = (hidden + part) // 2
    keep, send = call(
        functools.partial(item_gradient, scale, others),
        [out((kept, width)), out((kept, width))],
        [own_piece, own_grad, item_z, item_turned] + [back[step - 1] for step in ordered(others, (3, 2, 1))],
        flops=2 * rows * width * hidden,
    )
    swap = [(0, 1), (1, 0)]
    half = sum_over(keep + lax.ppermute(send, "sub", swap), "rep")
    direct = ring in (2, 4)
    if direct:
        half = half.astype(bf16)
        got = [lax.ppermute(half, "neg", pairs) for pairs in exchange]
        turns = ordered(others, (1, 3, 2))
        mine = call(
            functools.partial(add_pieces, turns, hidden // 2),
            [out((hidden, width), bf16)],
            [half] + [got[step - 1] for step in turns],
        )[0]
    else:
        item_half = lax.psum(half[: hidden // 2], "neg").astype(bf16)
        query_half = lax.all_gather(half[hidden // 2 :].astype(bf16), "neg", axis=0, tiled=True)
        mine = jnp.concatenate([item_half, query_half], axis=0)
    other = lax.ppermute(mine, "sub", swap)
    grad_query, grad_item = call(
        functools.partial(final_kernel, ring, direct),
        [out((hidden, width)), out((hidden, width))],
        [mine, other],
    )
    return (grad_query, grad_item, losses.reshape(count))


def solution(mesh):
    split = ("groups", "neg", "rep", "sub")
    return jax.shard_map(
        on_device,
        mesh=mesh,
        in_specs=(P(split, None), P(split, None), P(), P(), P(split), P(split), P(split)),
        out_specs=(P("groups", None), P("groups", None), P(split)),
        check_vma=False,
    )
```

```python
import functools
import math

import jax
import jax.numpy as jnp
from jax import lax
from jax.experimental import pallas as pl
from jax.experimental.pallas import tpu as pltpu
from jax.sharding import PartitionSpec as P

inverse_softness = 20.0
epsilon = 1e-06
log2e = math.log2(math.e)
ln2 = math.log(2.0)
tail_rows = 16
f32 = jnp.float32
bf16 = jnp.bfloat16


def contract(lhs, rhs, over):
    return lax.dot_general(lhs, rhs, (((over[0],), (over[1],)), ((), ())), preferred_element_type=f32)


def split_terms(values):
    terms = []
    for _ in range(3):
        term = values.astype(bf16).astype(f32)
        terms.append(term)
        values = values - term
    return terms


def item_tower(*refs):
    hbm, rest = refs[:7], refs[7:]
    message_ref, unit_ref, inverse_ref = rest[:3]
    targets = rest[3:6] + rest[7:9] + rest[6:7] + rest[9:10]
    sems = rest[10]
    copies = [pltpu.make_async_copy(source, target, sems.at[k]) for k, (source, target) in enumerate(zip(hbm, targets))]
    order = (5, 6, 3, 4, 0, 1, 2)
    for k in order:
        copies[k].start()
    feats_ref, proj_ref, ids_ref, counts_ref = targets[5], targets[6], targets[3], targets[4]
    rows = feats_ref.shape[0]
    copies[3].wait()
    copies[4].wait()
    ids = ids_ref[...]
    digits = [ids >> 16, (ids >> 8) & 255, ids & 255]
    log_counts = jnp.log(counts_ref[...].astype(f32)) * log2e
    lines = [digit.astype(f32) for digit in digits] + split_terms(log_counts)
    halves = ids.shape[0]
    lines.append(jnp.zeros((tail_rows - 6 * halves, ids.shape[1]), f32))
    message_ref[rows : rows + tail_rows, :] = jnp.concatenate(lines, axis=0).astype(bf16)
    copies[6].wait()
    copies[5].wait()
    z = jnp.dot(feats_ref[...], proj_ref[...], preferred_element_type=f32)
    inverse = 1.0 / jnp.sqrt(jnp.sum(z * z, axis=1, keepdims=True) + epsilon)
    unit = z * inverse
    message_ref[0:rows, :] = unit.astype(bf16)
    unit_ref[...] = unit
    inverse_ref[...] = jnp.broadcast_to(inverse, inverse_ref.shape)
    for k in (0, 1, 2):
        copies[k].wait()


def column_table(halves):
    line = lax.broadcasted_iota(jnp.int32, (tail_rows, 128), 0)
    parts = []
    for first, scales in ((0, (65536.0, 256.0, 1.0)), (3, (1.0, 1.0, 1.0))):
        for half in range(halves):
            part = jnp.zeros((tail_rows, 128), f32)
            for step, scale in enumerate(scales):
                part = jnp.where(line == (first + step) * halves + half, scale, part)
            parts.append(part)
    return jnp.concatenate(parts, axis=1).astype(bf16)


def item_columns(message_ref, table):
    rows = message_ref.shape[0] - tail_rows
    halves = rows // 128
    columns = contract(message_ref[rows : rows + tail_rows, :], table, (0, 0))
    ids = [columns[:, half * 128 : half * 128 + 128] for half in range(halves)]
    logs = [columns[:, (halves + half) * 128 : (halves + half) * 128 + 128] for half in range(halves)]
    return jnp.concatenate(ids, axis=0), jnp.concatenate(logs, axis=0)


def wide(column, width):
    return jnp.concatenate([column] * (width // column.shape[1]), axis=1)


def query_tower(
    feats_ref,
    proj_ref,
    message_ref,
    positives_ref,
    item_feats_ref,
    unit_ref,
    query_ref,
    plain_ref,
    weights_ref,
    weighted_ref,
    pos_ref,
    lines_ref,
    turned_ref,
    item_turned_ref,
    table_ref,
):
    rows = message_ref.shape[0] - tail_rows
    halves = rows // 128
    z = contract(proj_ref[...], feats_ref[...], (0, 1))
    inverse = 1.0 / jnp.sqrt(jnp.sum(z * z, axis=0, keepdims=True) + epsilon)
    scaled = z * inverse
    unit_ref[...] = scaled
    queries = scaled.astype(bf16)
    query_ref[...] = queries
    plain_ref[...] = queries.T
    count = queries.shape[1]
    positives = positives_ref[...]
    tail = message_ref[rows : rows + tail_rows, :]
    own = []
    pos_id = jnp.zeros((1, count), f32)
    for half in range(halves):
        spot = lax.broadcasted_iota(jnp.int32, (128, count), 0) + half * 128
        own.append(spot == positives)
        found = jnp.dot(tail, own[half].astype(f32).astype(bf16), preferred_element_type=f32)
        for step, scale in enumerate((65536.0, 256.0, 1.0)):
            line = step * halves + half
            pos_id = pos_id + scale * found[line : line + 1, :]
    table = column_table(halves)
    table_ref[...] = table
    own = jnp.concatenate(own, axis=0)
    items = message_ref[0:rows, :]
    ids, logs = item_columns(message_ref, table)
    scores = jnp.dot(items, queries, preferred_element_type=f32)
    scores = scores * (inverse_softness * log2e) - wide(logs, count)
    collide = (wide(ids, count) == pos_id) & jnp.logical_not(own)
    weights = jnp.where(collide, 0.0, jnp.exp2(scores))
    weights_ref[...] = weights
    totals = jnp.sum(weights, axis=0, keepdims=True)
    target = jnp.sum(jnp.where(own, scores, 0.0), axis=0, keepdims=True)
    weighted = contract(items, weights.astype(bf16), (0, 0))
    pos_items = contract(items, own.astype(f32).astype(bf16), (0, 0))
    weighted_ref[...] = weighted
    pos_ref[...] = pos_items
    lines_ref[...] = jnp.concatenate([totals, target * ln2, pos_id, inverse, jnp.zeros((4, count), f32)], axis=0)
    turned_ref[...] = feats_ref[...].T
    item_turned_ref[...] = item_feats_ref[...].T


def add_block(message_ref, query_ref, lines_ref, table_ref, before_ref, totals, weights_ref, chunk=32):
    rows, count = weights_ref.shape
    pos_id = lines_ref[2:3, :]
    partial = jnp.zeros((8, count), f32)
    items = message_ref[0:rows, :]
    ids, logs = item_columns(message_ref, table_ref[...])
    scores = jnp.dot(items, query_ref[...], preferred_element_type=f32)
    rounded = []
    for first in range(0, rows, chunk):
        part = slice(first, first + chunk)
        exponent = scores[part] * (inverse_softness * log2e) - wide(logs[part], count)
        weights = jnp.where(wide(ids[part], count) == pos_id, 0.0, jnp.exp2(exponent))
        for line in range(0, chunk, 8):
            partial = partial + weights[line : line + 8]
        rounded.append(weights.astype(bf16))
    rounded = jnp.concatenate(rounded, axis=0)
    weights_ref[...] = rounded
    weighted = before_ref[...] + contract(items, rounded, (0, 0))
    return totals + jnp.sum(partial, axis=0, keepdims=True), weighted


def middle_block(message_ref, query_ref, lines_ref, table_ref, before_ref, totals_ref, weights_ref, after_ref, sums_ref):
    totals, weighted = add_block(message_ref, query_ref, lines_ref, table_ref, before_ref, totals_ref[0:1, :], weights_ref)
    after_ref[...] = weighted
    sums_ref[...] = jnp.broadcast_to(totals, sums_ref.shape)


def last_block(scale, others, ring, chain, *refs):
    (
        message_ref,
        query_ref,
        plain_ref,
        lines_ref,
        table_ref,
        before_ref,
        totals_ref,
        positives_ref,
        own_weights_ref,
        pos_ref,
        unit_ref,
        turned_ref,
    ) = refs[:12]
    weights_refs = refs[12 : 11 + others]
    piece_refs = refs[11 + others : 11 + 2 * others]
    own_ref, own_grad_ref, losses_ref, last_ref, grad_ref = refs[11 + 2 * others :]
    rows, count = own_weights_ref.shape
    totals, weighted = add_block(message_ref, query_ref, lines_ref, table_ref, before_ref, totals_ref[0:1, :], last_ref)
    losses_ref[...] = jnp.log(totals) - lines_ref[1:2, :]
    share = 1.0 / totals
    cot = weighted * share - pos_ref[...]
    unit = unit_ref[...]
    along = jnp.sum(unit * cot, axis=0, keepdims=True)
    dz = ((cot - unit * along) * (lines_ref[3:4, :] * scale)).astype(bf16)
    shared = (query_ref[...].astype(f32) * share).astype(bf16)
    for step, weights_ref in zip(chain, list(weights_refs) + [last_ref]):
        piece_refs[step - 1][0:rows, :] = contract(weights_ref[...], shared, (1, 1)).astype(bf16)
    own = lax.broadcasted_iota(jnp.int32, (rows, count), 0) == positives_ref[...]
    grads = (own_weights_ref[...] * share - own.astype(f32)).astype(bf16)
    own_ref[...] = jnp.dot(grads, plain_ref[...], preferred_element_type=f32)
    grad_ref[...] = contract(turned_ref[...], dz, (1, 1))
    me = lax.axis_index("neg")
    part = grad_ref.shape[0] // ring
    own_grad_ref[...] = grad_ref[pl.ds(pl.multiple_of(me * part, part), part), :]
    for step, piece_ref in enumerate(piece_refs):
        target = source_of(me, step + 1, ring)
        piece_ref[rows : rows + part, :] = grad_ref[pl.ds(pl.multiple_of(target * part, part), part), :].astype(bf16)


def item_gradient(scale, others, own_ref, own_grad_ref, unit_ref, inverse_ref, turned_ref, *refs):
    keep_ref, send_ref = refs[others:]
    rows = own_ref.shape[0]
    cot = own_ref[...]
    query_grad = own_grad_ref[...]
    for ref in refs[:others]:
        cot = cot + ref[0:rows, :].astype(f32)
        query_grad = query_grad + ref[rows:, :].astype(f32)
    unit = unit_ref[...]
    along = jnp.sum(unit * cot, axis=1, keepdims=True)
    dz = ((cot - unit * along) * (inverse_ref[...] * scale)).astype(bf16)
    grad = jnp.dot(turned_ref[...], dz, preferred_element_type=f32)
    first = lax.axis_index("sub") == 0
    for start, whole in ((0, grad), (grad.shape[0] // 2, query_grad)):
        half = whole.shape[0] // 2
        keep_ref[start : start + half, :] = jnp.where(first, whole[:half], whole[half:])
        send_ref[start : start + half, :] = jnp.where(first, whole[half:], whole[:half])


def add_pieces(turns, item_rows, own_ref, *refs):
    out_ref = refs[-1]
    values = [own_ref[...].astype(f32)]
    for step in range(1, len(turns) + 1):
        values.append(refs[turns.index(step)][...].astype(f32))
    total = values[0] + values[1]
    if len(values) == 4:
        total = total + (values[2] + values[3])
    query_rows = own_ref.shape[0] - item_rows
    out_ref[0:item_rows, :] = total[:item_rows].astype(bf16)
    for step, value in enumerate(values):
        start = item_rows + step * query_rows
        out_ref[start : start + query_rows, :] = value[item_rows:].astype(bf16)


def place_kernel(ring, direct, other, *refs):
    values_ref = refs[0]
    query_hbm, item_hbm, wide_ref, sems = refs[-4:]
    sub = lax.axis_index("sub")
    side = 1 - sub if other else sub
    base = lax.axis_index("neg") if direct else 0
    half = item_hbm.shape[0] // 2
    part = half // ring
    wide_ref[...] = values_ref[...].astype(f32)
    copies = [
        pltpu.make_async_copy(
            wide_ref.at[pl.ds(0, half)], item_hbm.at[pl.ds(pl.multiple_of(side * half, half), half)], sems.at[ring]
        )
    ]
    for step in range(ring):
        start = pl.multiple_of(partner_of(base, step, ring) * (2 * part) + side * part, part)
        copies.append(
            pltpu.make_async_copy(
                wide_ref.at[pl.ds(half + step * part, part)], query_hbm.at[pl.ds(start, part)], sems.at[step]
            )
        )
    for copy in copies:
        copy.start()
    for copy in copies:
        copy.wait()


def place(ring, direct, other, values, outs):
    hbm = pl.BlockSpec(memory_space=pltpu.HBM)
    shape = jax.ShapeDtypeStruct(values.shape, f32)
    return pl.pallas_call(
        functools.partial(place_kernel, ring, direct, other),
        out_shape=(shape, shape),
        in_specs=[pl.BlockSpec(memory_space=pltpu.VMEM)] + [hbm] * len(outs),
        out_specs=(hbm, hbm),
        input_output_aliases={1: 0, 2: 1} if outs else {},
        scratch_shapes=[pltpu.VMEM(values.shape, f32), pltpu.SemaphoreType.DMA((ring + 1,))],
        compiler_params=pltpu.CompilerParams(vmem_limit_bytes=32 * 1024 * 1024),
        cost_estimate=pl.CostEstimate(flops=0, bytes_accessed=6 * values.size, transcendentals=0),
    )(values, *outs)


def call(kernel, outs, args, scratch=(), flops=0, fetch=False, room=32):
    vmem = pl.BlockSpec(memory_space=pltpu.VMEM)
    moved = sum(math.prod(s.shape) * s.dtype.itemsize for s in list(outs) + list(args))
    return pl.pallas_call(
        kernel,
        out_shape=tuple(jax.ShapeDtypeStruct(s.shape, s.dtype) for s in outs),
        in_specs=[pl.BlockSpec(memory_space=pltpu.HBM) if fetch else vmem] * len(args),
        out_specs=tuple([vmem] * len(outs)),
        scratch_shapes=list(scratch),
        compiler_params=pltpu.CompilerParams(vmem_limit_bytes=room * 1024 * 1024),
        cost_estimate=pl.CostEstimate(flops=flops, bytes_accessed=moved, transcendentals=0),
    )(*args)


def pin(values):
    return pltpu.with_memory_space_constraint(values, pltpu.HBM)


def out(shape, dtype=f32):
    return jax.ShapeDtypeStruct(shape, dtype)


def partner_of(me, step, count):
    if count & (count - 1) == 0:
        return me ^ step
    return lax.rem(me + step, count)


def source_of(me, step, count):
    return partner_of(me, step if count & (count - 1) == 0 else count - step, count)


def partners(count):
    return [[(j, int(partner_of(j, step, count))) for j in range(count)] for step in range(1, count)]


def ordered(others, order):
    return list(order) if len(order) == others else list(range(1, others + 1))


def sent_back(pairs):
    return [(target, source) for source, target in pairs]


def sum_over(values, axis):
    size = lax.axis_size(axis)
    if size == 1:
        return values
    if size not in (2, 4):
        return lax.psum(values, axis)
    values = values.astype(bf16)
    got = [lax.ppermute(values, axis, pairs).astype(f32) for pairs in partners(size)]
    total = values.astype(f32) + got[0]
    return total + (got[1] + got[2]) if size == 4 else total


def on_device(query_feats, item_feats, query_proj, item_proj, item_ids, item_counts, positives):
    count, hidden = query_feats.shape
    rows = item_feats.shape[0]
    width = query_proj.shape[1]
    scale = inverse_softness / count
    halves = rows // 128
    ring = lax.axis_size("neg")
    exchange = partners(ring)
    others = len(exchange)
    part = hidden // ring
    message, item_unit, item_inverse, query_feats, query_proj, spots, item_feats = call(
        item_tower,
        [
            out((rows + tail_rows, width), bf16),
            out((rows, width)),
            out((rows, width)),
            out((count, hidden), bf16),
            out((hidden, width), bf16),
            out((1, count), jnp.int32),
            out((rows, hidden), bf16),
        ],
        [
            pin(query_feats),
            pin(query_proj),
            pin(positives.reshape(1, count)),
            pin(item_ids.reshape(halves, 128)),
            pin(item_counts.reshape(halves, 128)),
            pin(item_feats),
            pin(item_proj),
        ],
        scratch=[
            pltpu.VMEM((halves, 128), jnp.int32),
            pltpu.VMEM((halves, 128), jnp.int32),
            pltpu.VMEM((hidden, width), bf16),
            pltpu.SemaphoreType.DMA((7,)),
        ],
        flops=2 * rows * hidden * width,
        fetch=True,
        room=32,
    )
    received = [lax.ppermute(message, "neg", pairs) for pairs in exchange]
    query_unit, queries, plain, own_weights, weighted, pos_items, lines, turned, item_turned, table = call(
        query_tower,
        [
            out((width, count)),
            out((width, count), bf16),
            out((count, width), bf16),
            out((rows, count)),
            out((width, count)),
            out((width, count)),
            out((8, count)),
            out((hidden, count), bf16),
            out((hidden, rows), bf16),
            out((tail_rows, 2 * rows), bf16),
        ],
        [query_feats, query_proj, message, spots, item_feats],
        flops=2 * count * width * (hidden + 3 * rows),
    )
    totals = lines
    weights = []
    chain = ordered(others, (1, 2, 3))
    for step in chain[:-1]:
        block = received[step - 1]
        block_weights, weighted, totals = call(
            middle_block,
            [out((rows, count), bf16), out((width, count)), out((8, count))],
            [block, queries, lines, table, weighted, totals],
            flops=4 * count * width * rows,
        )
        weights.append(block_weights)
    results = call(
        functools.partial(last_block, scale, others, ring, chain),
        [out((rows + part, width), bf16)] * others + [out((rows, width)), out((part, width)), out((1, count))],
        [received[chain[-1] - 1], queries, plain, lines, table, weighted, totals, spots, own_weights, pos_items, query_unit, turned] + weights,
        scratch=[pltpu.VMEM((rows, count), bf16), pltpu.VMEM((hidden, width), f32)],
        flops=6 * count * width * rows * (others + 1),
    )
    own_piece, own_grad, losses = results[others:]
    back = [lax.ppermute(piece, "neg", sent_back(pairs)) for piece, pairs in zip(results, exchange)]
    kept = (hidden + part) // 2
    keep, send = call(
        functools.partial(item_gradient, scale, others),
        [out((kept, width)), out((kept, width))],
        [own_piece, own_grad, item_unit, item_inverse, item_turned] + [back[step - 1] for step in ordered(others, (3, 2, 1))],
        flops=2 * rows * width * hidden,
    )
    swap = [(0, 1), (1, 0)]
    half = sum_over(keep + lax.ppermute(send, "sub", swap), "rep")
    direct = ring in (2, 4)
    if direct:
        half = half.astype(bf16)
        got = [lax.ppermute(half, "neg", pairs) for pairs in exchange]
        turns = ordered(others, (3, 1, 2))
        mine = call(
            functools.partial(add_pieces, turns, hidden // 2),
            [out((hidden, width), bf16)],
            [half] + [got[step - 1] for step in turns],
        )[0]
    else:
        item_half = lax.psum(half[: hidden // 2], "neg").astype(bf16)
        query_half = lax.all_gather(half[hidden // 2 :].astype(bf16), "neg", axis=0, tiled=True)
        mine = jnp.concatenate([item_half, query_half], axis=0)
    other = lax.ppermute(mine, "sub", swap)
    outs = place(ring, direct, False, mine, ())
    grad_query, grad_item = place(ring, direct, True, other, outs)
    return (grad_query, grad_item, losses.reshape(count))


def solution(mesh):
    split = ("groups", "neg", "rep", "sub")
    return jax.shard_map(
        on_device,
        mesh=mesh,
        in_specs=(P(split, None), P(split, None), P(), P(), P(split), P(split), P(split)),
        out_specs=(P("groups", None), P("groups", None), P(split)),
        check_vma=False,
    )
```

```python
import functools
import math

import jax
import jax.numpy as jnp
from jax import lax
from jax.experimental import pallas as pl
from jax.experimental.pallas import tpu as pltpu
from jax.sharding import PartitionSpec as P

inverse_softness = 20.0
epsilon = 1e-06
log2e = math.log2(math.e)
ln2 = math.log(2.0)
tail_rows = 16
f32 = jnp.float32
bf16 = jnp.bfloat16


def contract(lhs, rhs, over):
    return lax.dot_general(lhs, rhs, (((over[0],), (over[1],)), ((), ())), preferred_element_type=f32)


def split_terms(values):
    terms = []
    for _ in range(3):
        term = values.astype(bf16).astype(f32)
        terms.append(term)
        values = values - term
    return terms


def item_tower(*refs):
    hbm, rest = refs[:7], refs[7:]
    message_ref, unit_ref, inverse_ref = rest[:3]
    targets = rest[3:6] + rest[7:9] + rest[6:7] + rest[9:10]
    sems = rest[10]
    copies = [pltpu.make_async_copy(source, target, sems.at[k]) for k, (source, target) in enumerate(zip(hbm, targets))]
    order = (5, 6, 3, 4, 0, 1, 2)
    for k in order:
        copies[k].start()
    feats_ref, proj_ref, ids_ref, counts_ref = targets[5], targets[6], targets[3], targets[4]
    rows = feats_ref.shape[0]
    copies[3].wait()
    copies[4].wait()
    ids = ids_ref[...]
    digits = [ids >> 16, (ids >> 8) & 255, ids & 255]
    log_counts = jnp.log(counts_ref[...].astype(f32)) * log2e
    lines = [digit.astype(f32) for digit in digits] + split_terms(log_counts)
    halves = ids.shape[0]
    lines.append(jnp.zeros((tail_rows - 6 * halves, ids.shape[1]), f32))
    message_ref[rows : rows + tail_rows, :] = jnp.concatenate(lines, axis=0).astype(bf16)
    copies[6].wait()
    copies[5].wait()
    z = jnp.dot(feats_ref[...], proj_ref[...], preferred_element_type=f32)
    inverse = 1.0 / jnp.sqrt(jnp.sum(z * z, axis=1, keepdims=True) + epsilon)
    unit = z * inverse
    message_ref[0:rows, :] = unit.astype(bf16)
    unit_ref[...] = unit
    inverse_ref[...] = jnp.broadcast_to(inverse, inverse_ref.shape)
    for k in (0, 1, 2):
        copies[k].wait()


def column_table(halves):
    line = lax.broadcasted_iota(jnp.int32, (tail_rows, 128), 0)
    parts = []
    for first, scales in ((0, (65536.0, 256.0, 1.0)), (3, (1.0, 1.0, 1.0))):
        for half in range(halves):
            part = jnp.zeros((tail_rows, 128), f32)
            for step, scale in enumerate(scales):
                part = jnp.where(line == (first + step) * halves + half, scale, part)
            parts.append(part)
    return jnp.concatenate(parts, axis=1).astype(bf16)


def item_columns(message_ref, table):
    rows = message_ref.shape[0] - tail_rows
    halves = rows // 128
    columns = contract(message_ref[rows : rows + tail_rows, :], table, (0, 0))
    ids = [columns[:, half * 128 : half * 128 + 128] for half in range(halves)]
    logs = [columns[:, (halves + half) * 128 : (halves + half) * 128 + 128] for half in range(halves)]
    return jnp.concatenate(ids, axis=0), jnp.concatenate(logs, axis=0)


def wide(column, width):
    return jnp.concatenate([column] * (width // column.shape[1]), axis=1)


def query_tower(
    feats_ref,
    proj_ref,
    message_ref,
    positives_ref,
    item_feats_ref,
    unit_ref,
    query_ref,
    plain_ref,
    weights_ref,
    weighted_ref,
    pos_ref,
    lines_ref,
    turned_ref,
    item_turned_ref,
    table_ref,
):
    rows = message_ref.shape[0] - tail_rows
    halves = rows // 128
    z = contract(proj_ref[...], feats_ref[...], (0, 1))
    inverse = 1.0 / jnp.sqrt(jnp.sum(z * z, axis=0, keepdims=True) + epsilon)
    scaled = z * inverse
    unit_ref[...] = scaled
    queries = scaled.astype(bf16)
    query_ref[...] = queries
    plain_ref[...] = queries.T
    count = queries.shape[1]
    positives = positives_ref[...]
    tail = message_ref[rows : rows + tail_rows, :]
    own = []
    pos_id = jnp.zeros((1, count), f32)
    for half in range(halves):
        spot = lax.broadcasted_iota(jnp.int32, (128, count), 0) + half * 128
        own.append(spot == positives)
        found = jnp.dot(tail, own[half].astype(f32).astype(bf16), preferred_element_type=f32)
        for step, scale in enumerate((65536.0, 256.0, 1.0)):
            line = step * halves + half
            pos_id = pos_id + scale * found[line : line + 1, :]
    table = column_table(halves)
    table_ref[...] = table
    own = jnp.concatenate(own, axis=0)
    items = message_ref[0:rows, :]
    ids, logs = item_columns(message_ref, table)
    scores = jnp.dot(items, queries, preferred_element_type=f32)
    scores = scores * (inverse_softness * log2e) - wide(logs, count)
    collide = (wide(ids, count) == pos_id) & jnp.logical_not(own)
    weights = jnp.where(collide, 0.0, jnp.exp2(scores))
    weights_ref[...] = weights
    totals = jnp.sum(weights, axis=0, keepdims=True)
    target = jnp.sum(jnp.where(own, scores, 0.0), axis=0, keepdims=True)
    weighted = contract(items, weights.astype(bf16), (0, 0))
    pos_items = contract(items, own.astype(f32).astype(bf16), (0, 0))
    weighted_ref[...] = weighted
    pos_ref[...] = pos_items
    lines_ref[...] = jnp.concatenate([totals, target * ln2, pos_id, inverse, jnp.zeros((4, count), f32)], axis=0)
    turned_ref[...] = feats_ref[...].T
    item_turned_ref[...] = item_feats_ref[...].T


def add_block(message_ref, query_ref, lines_ref, table_ref, before_ref, totals, weights_ref, chunk=32):
    rows, count = weights_ref.shape
    pos_id = lines_ref[2:3, :]
    partial = jnp.zeros((8, count), f32)
    items = message_ref[0:rows, :]
    ids, logs = item_columns(message_ref, table_ref[...])
    scores = jnp.dot(items, query_ref[...], preferred_element_type=f32)
    rounded = []
    for first in range(0, rows, chunk):
        part = slice(first, first + chunk)
        exponent = scores[part] * (inverse_softness * log2e) - wide(logs[part], count)
        weights = jnp.where(wide(ids[part], count) == pos_id, 0.0, jnp.exp2(exponent))
        for line in range(0, chunk, 8):
            partial = partial + weights[line : line + 8]
        rounded.append(weights.astype(bf16))
    rounded = jnp.concatenate(rounded, axis=0)
    weights_ref[...] = rounded
    weighted = before_ref[...] + contract(items, rounded, (0, 0))
    return totals + jnp.sum(partial, axis=0, keepdims=True), weighted


def middle_block(message_ref, query_ref, lines_ref, table_ref, before_ref, totals_ref, weights_ref, after_ref, sums_ref):
    totals, weighted = add_block(message_ref, query_ref, lines_ref, table_ref, before_ref, totals_ref[0:1, :], weights_ref)
    after_ref[...] = weighted
    sums_ref[...] = jnp.broadcast_to(totals, sums_ref.shape)


def last_block(scale, others, ring, chain, *refs):
    (
        message_ref,
        query_ref,
        lines_ref,
        table_ref,
        before_ref,
        totals_ref,
        pos_ref,
        unit_ref,
        turned_ref,
    ) = refs[:9]
    weights_refs = refs[9 : 8 + others]
    piece_refs = refs[8 + others : 8 + 2 * others]
    own_grad_ref, sums_ref, last_ref, grad_ref = refs[8 + 2 * others :]
    rows, count = last_ref.shape
    totals, weighted = add_block(message_ref, query_ref, lines_ref, table_ref, before_ref, totals_ref[0:1, :], last_ref)
    share = 1.0 / totals
    sums_ref[...] = jnp.concatenate([totals, share, jnp.zeros((6, count), f32)], axis=0)
    cot = weighted * share - pos_ref[...]
    unit = unit_ref[...]
    along = jnp.sum(unit * cot, axis=0, keepdims=True)
    dz = ((cot - unit * along) * (lines_ref[3:4, :] * scale)).astype(bf16)
    shared = (query_ref[...].astype(f32) * share).astype(bf16)
    for step, weights_ref in zip(chain, list(weights_refs) + [last_ref]):
        piece_refs[step - 1][0:rows, :] = contract(weights_ref[...], shared, (1, 1)).astype(bf16)
    grad_ref[...] = contract(turned_ref[...], dz, (1, 1))
    me = lax.axis_index("neg")
    part = grad_ref.shape[0] // ring
    own_grad_ref[...] = grad_ref[pl.ds(pl.multiple_of(me * part, part), part), :]
    for step, piece_ref in enumerate(piece_refs):
        target = source_of(me, step + 1, ring)
        piece_ref[rows : rows + part, :] = grad_ref[pl.ds(pl.multiple_of(target * part, part), part), :].astype(bf16)


def own_block(sums_ref, lines_ref, positives_ref, weights_ref, plain_ref, own_ref, losses_ref):
    losses_ref[...] = jnp.log(sums_ref[0:1, :]) - lines_ref[1:2, :]
    own = lax.broadcasted_iota(jnp.int32, weights_ref.shape, 0) == positives_ref[...]
    grads = (weights_ref[...] * sums_ref[1:2, :] - own.astype(f32)).astype(bf16)
    own_ref[...] = jnp.dot(grads, plain_ref[...], preferred_element_type=f32)


def item_gradient(scale, others, own_ref, own_grad_ref, unit_ref, inverse_ref, turned_ref, *refs):
    keep_ref, send_ref = refs[others:]
    rows = own_ref.shape[0]
    cot = own_ref[...]
    query_grad = own_grad_ref[...]
    for ref in refs[:others]:
        cot = cot + ref[0:rows, :].astype(f32)
        query_grad = query_grad + ref[rows:, :].astype(f32)
    unit = unit_ref[...]
    along = jnp.sum(unit * cot, axis=1, keepdims=True)
    dz = ((cot - unit * along) * (inverse_ref[...] * scale)).astype(bf16)
    grad = jnp.dot(turned_ref[...], dz, preferred_element_type=f32)
    first = lax.axis_index("sub") == 0
    for start, whole in ((0, grad), (grad.shape[0] // 2, query_grad)):
        half = whole.shape[0] // 2
        keep_ref[start : start + half, :] = jnp.where(first, whole[:half], whole[half:])
        send_ref[start : start + half, :] = jnp.where(first, whole[half:], whole[:half])


def add_pieces(turns, item_rows, own_ref, *refs):
    out_ref = refs[-1]
    values = [own_ref[...].astype(f32)]
    for step in range(1, len(turns) + 1):
        values.append(refs[turns.index(step)][...].astype(f32))
    total = values[0] + values[1]
    if len(values) == 4:
        total = total + (values[2] + values[3])
    query_rows = own_ref.shape[0] - item_rows
    out_ref[0:item_rows, :] = total[:item_rows].astype(bf16)
    for step, value in enumerate(values):
        start = item_rows + step * query_rows
        out_ref[start : start + query_rows, :] = value[item_rows:].astype(bf16)


def place_kernel(ring, direct, other, *refs):
    values_ref = refs[0]
    query_hbm, item_hbm, wide_ref, sems = refs[-4:]
    sub = lax.axis_index("sub")
    side = 1 - sub if other else sub
    base = lax.axis_index("neg") if direct else 0
    half = item_hbm.shape[0] // 2
    part = half // ring
    wide_ref[...] = values_ref[...].astype(f32)
    copies = [
        pltpu.make_async_copy(
            wide_ref.at[pl.ds(0, half)], item_hbm.at[pl.ds(pl.multiple_of(side * half, half), half)], sems.at[ring]
        )
    ]
    for step in range(ring):
        start = pl.multiple_of(partner_of(base, step, ring) * (2 * part) + side * part, part)
        copies.append(
            pltpu.make_async_copy(
                wide_ref.at[pl.ds(half + step * part, part)], query_hbm.at[pl.ds(start, part)], sems.at[step]
            )
        )
    for copy in copies:
        copy.start()
    for copy in copies:
        copy.wait()


def place(ring, direct, other, values, outs):
    hbm = pl.BlockSpec(memory_space=pltpu.HBM)
    shape = jax.ShapeDtypeStruct(values.shape, f32)
    return pl.pallas_call(
        functools.partial(place_kernel, ring, direct, other),
        out_shape=(shape, shape),
        in_specs=[pl.BlockSpec(memory_space=pltpu.VMEM)] + [hbm] * len(outs),
        out_specs=(hbm, hbm),
        input_output_aliases={1: 0, 2: 1} if outs else {},
        scratch_shapes=[pltpu.VMEM(values.shape, f32), pltpu.SemaphoreType.DMA((ring + 1,))],
        compiler_params=pltpu.CompilerParams(vmem_limit_bytes=32 * 1024 * 1024),
        cost_estimate=pl.CostEstimate(flops=0, bytes_accessed=6 * values.size, transcendentals=0),
    )(values, *outs)


def call(kernel, outs, args, scratch=(), flops=0, fetch=False, room=32):
    vmem = pl.BlockSpec(memory_space=pltpu.VMEM)
    moved = sum(math.prod(s.shape) * s.dtype.itemsize for s in list(outs) + list(args))
    return pl.pallas_call(
        kernel,
        out_shape=tuple(jax.ShapeDtypeStruct(s.shape, s.dtype) for s in outs),
        in_specs=[pl.BlockSpec(memory_space=pltpu.HBM) if fetch else vmem] * len(args),
        out_specs=tuple([vmem] * len(outs)),
        scratch_shapes=list(scratch),
        compiler_params=pltpu.CompilerParams(vmem_limit_bytes=room * 1024 * 1024),
        cost_estimate=pl.CostEstimate(flops=flops, bytes_accessed=moved, transcendentals=0),
    )(*args)


def pin(values):
    return pltpu.with_memory_space_constraint(values, pltpu.HBM)


def out(shape, dtype=f32):
    return jax.ShapeDtypeStruct(shape, dtype)


def partner_of(me, step, count):
    if count & (count - 1) == 0:
        return me ^ step
    return lax.rem(me + step, count)


def source_of(me, step, count):
    return partner_of(me, step if count & (count - 1) == 0 else count - step, count)


def partners(count):
    return [[(j, int(partner_of(j, step, count))) for j in range(count)] for step in range(1, count)]


def ordered(others, order):
    return list(order) if len(order) == others else list(range(1, others + 1))


def sent_back(pairs):
    return [(target, source) for source, target in pairs]


def sum_over(values, axis):
    size = lax.axis_size(axis)
    if size == 1:
        return values
    if size not in (2, 4):
        return lax.psum(values, axis)
    values = values.astype(bf16)
    got = [lax.ppermute(values, axis, pairs).astype(f32) for pairs in partners(size)]
    total = values.astype(f32) + got[0]
    return total + (got[1] + got[2]) if size == 4 else total


def on_device(query_feats, item_feats, query_proj, item_proj, item_ids, item_counts, positives):
    count, hidden = query_feats.shape
    rows = item_feats.shape[0]
    width = query_proj.shape[1]
    scale = inverse_softness / count
    halves = rows // 128
    ring = lax.axis_size("neg")
    exchange = partners(ring)
    others = len(exchange)
    part = hidden // ring
    message, item_unit, item_inverse, query_feats, query_proj, spots, item_feats = call(
        item_tower,
        [
            out((rows + tail_rows, width), bf16),
            out((rows, width)),
            out((rows, width)),
            out((count, hidden), bf16),
            out((hidden, width), bf16),
            out((1, count), jnp.int32),
            out((rows, hidden), bf16),
        ],
        [
            pin(query_feats),
            pin(query_proj),
            pin(positives.reshape(1, count)),
            pin(item_ids.reshape(halves, 128)),
            pin(item_counts.reshape(halves, 128)),
            pin(item_feats),
            pin(item_proj),
        ],
        scratch=[
            pltpu.VMEM((halves, 128), jnp.int32),
            pltpu.VMEM((halves, 128), jnp.int32),
            pltpu.VMEM((hidden, width), bf16),
            pltpu.SemaphoreType.DMA((7,)),
        ],
        flops=2 * rows * hidden * width,
        fetch=True,
        room=32,
    )
    received = [lax.ppermute(message, "neg", pairs) for pairs in exchange]
    query_unit, queries, plain, own_weights, weighted, pos_items, lines, turned, item_turned, table = call(
        query_tower,
        [
            out((width, count)),
            out((width, count), bf16),
            out((count, width), bf16),
            out((rows, count)),
            out((width, count)),
            out((width, count)),
            out((8, count)),
            out((hidden, count), bf16),
            out((hidden, rows), bf16),
            out((tail_rows, 2 * rows), bf16),
        ],
        [query_feats, query_proj, message, spots, item_feats],
        flops=2 * count * width * (hidden + 3 * rows),
    )
    totals = lines
    weights = []
    chain = ordered(others, (1, 2, 3))
    for step in chain[:-1]:
        block = received[step - 1]
        block_weights, weighted, totals = call(
            middle_block,
            [out((rows, count), bf16), out((width, count)), out((8, count))],
            [block, queries, lines, table, weighted, totals],
            flops=4 * count * width * rows,
        )
        weights.append(block_weights)
    results = call(
        functools.partial(last_block, scale, others, ring, chain),
        [out((rows + part, width), bf16)] * others + [out((part, width)), out((8, count))],
        [received[chain[-1] - 1], queries, lines, table, weighted, totals, pos_items, query_unit, turned] + weights,
        scratch=[pltpu.VMEM((rows, count), bf16), pltpu.VMEM((hidden, width), f32)],
        flops=6 * count * width * rows * (others + 1),
    )
    own_grad, sums = results[others:]
    back = [lax.ppermute(piece, "neg", sent_back(pairs)) for piece, pairs in zip(results, exchange)]
    own_piece, losses = call(
        own_block,
        [out((rows, width)), out((1, count))],
        [sums, lines, spots, own_weights, plain],
        flops=2 * rows * width * count,
    )
    kept = (hidden + part) // 2
    keep, send = call(
        functools.partial(item_gradient, scale, others),
        [out((kept, width)), out((kept, width))],
        [own_piece, own_grad, item_unit, item_inverse, item_turned] + [back[step - 1] for step in ordered(others, (3, 2, 1))],
        flops=2 * rows * width * hidden,
    )
    swap = [(0, 1), (1, 0)]
    half = sum_over(keep + lax.ppermute(send, "sub", swap), "rep")
    direct = ring in (2, 4)
    if direct:
        half = half.astype(bf16)
        got = [lax.ppermute(half, "neg", pairs) for pairs in exchange]
        turns = ordered(others, (3, 1, 2))
        mine = call(
            functools.partial(add_pieces, turns, hidden // 2),
            [out((hidden, width), bf16)],
            [half] + [got[step - 1] for step in turns],
        )[0]
    else:
        item_half = lax.psum(half[: hidden // 2], "neg").astype(bf16)
        query_half = lax.all_gather(half[hidden // 2 :].astype(bf16), "neg", axis=0, tiled=True)
        mine = jnp.concatenate([item_half, query_half], axis=0)
    other = lax.ppermute(mine, "sub", swap)
    outs = place(ring, direct, False, mine, ())
    grad_query, grad_item = place(ring, direct, True, other, outs)
    return (grad_query, grad_item, losses.reshape(count))


def solution(mesh):
    split = ("groups", "neg", "rep", "sub")
    return jax.shard_map(
        on_device,
        mesh=mesh,
        in_specs=(P(split, None), P(split, None), P(), P(), P(split), P(split), P(split)),
        out_specs=(P("groups", None), P("groups", None), P(split)),
        check_vma=False,
    )
```

```python
import functools
import math

import jax
import jax.numpy as jnp
from jax import lax
from jax.experimental import pallas as pl
from jax.experimental.pallas import tpu as pltpu
from jax.sharding import PartitionSpec as P

inverse_softness = 20.0
epsilon = 1e-06
log2e = math.log2(math.e)
ln2 = math.log(2.0)
tail_rows = 16
f32 = jnp.float32
bf16 = jnp.bfloat16


def contract(lhs, rhs, over):
    return lax.dot_general(lhs, rhs, (((over[0],), (over[1],)), ((), ())), preferred_element_type=f32)


def split_terms(values):
    terms = []
    for _ in range(3):
        term = values.astype(bf16).astype(f32)
        terms.append(term)
        values = values - term
    return terms


def item_tower(*refs):
    hbm, rest = refs[:7], refs[7:]
    message_ref, unit_ref, inverse_ref = rest[:3]
    targets = rest[3:6] + rest[7:9] + rest[6:7] + rest[9:10]
    sems = rest[10]
    copies = [pltpu.make_async_copy(source, target, sems.at[k]) for k, (source, target) in enumerate(zip(hbm, targets))]
    order = (5, 6, 3, 4, 0, 1, 2)
    for k in order:
        copies[k].start()
    feats_ref, proj_ref, ids_ref, counts_ref = targets[5], targets[6], targets[3], targets[4]
    rows = feats_ref.shape[0]
    copies[3].wait()
    copies[4].wait()
    ids = ids_ref[...]
    digits = [ids >> 16, (ids >> 8) & 255, ids & 255]
    log_counts = jnp.log(counts_ref[...].astype(f32)) * log2e
    lines = [digit.astype(f32) for digit in digits] + split_terms(log_counts)
    halves = ids.shape[0]
    lines.append(jnp.zeros((tail_rows - 6 * halves, ids.shape[1]), f32))
    message_ref[rows : rows + tail_rows, :] = jnp.concatenate(lines, axis=0).astype(bf16)
    copies[6].wait()
    copies[5].wait()
    z = jnp.dot(feats_ref[...], proj_ref[...], preferred_element_type=f32)
    inverse = 1.0 / jnp.sqrt(jnp.sum(z * z, axis=1, keepdims=True) + epsilon)
    unit = z * inverse
    message_ref[0:rows, :] = unit.astype(bf16)
    unit_ref[...] = unit
    inverse_ref[...] = jnp.broadcast_to(inverse, inverse_ref.shape)
    for k in (0, 1, 2):
        copies[k].wait()


def column_table(halves):
    line = lax.broadcasted_iota(jnp.int32, (tail_rows, 128), 0)
    parts = []
    for first, scales in ((0, (65536.0, 256.0, 1.0)), (3, (1.0, 1.0, 1.0))):
        for half in range(halves):
            part = jnp.zeros((tail_rows, 128), f32)
            for step, scale in enumerate(scales):
                part = jnp.where(line == (first + step) * halves + half, scale, part)
            parts.append(part)
    return jnp.concatenate(parts, axis=1).astype(bf16)


def item_columns(message_ref, table):
    rows = message_ref.shape[0] - tail_rows
    halves = rows // 128
    columns = contract(message_ref[rows : rows + tail_rows, :], table, (0, 0))
    ids = [columns[:, half * 128 : half * 128 + 128] for half in range(halves)]
    logs = [columns[:, (halves + half) * 128 : (halves + half) * 128 + 128] for half in range(halves)]
    return jnp.concatenate(ids, axis=0), jnp.concatenate(logs, axis=0)


def wide(column, width):
    return jnp.concatenate([column] * (width // column.shape[1]), axis=1)


def query_tower(
    feats_ref,
    proj_ref,
    message_ref,
    positives_ref,
    item_feats_ref,
    unit_ref,
    query_ref,
    plain_ref,
    weights_ref,
    weighted_ref,
    pos_ref,
    lines_ref,
    turned_ref,
    item_turned_ref,
    table_ref,
):
    rows = message_ref.shape[0] - tail_rows
    halves = rows // 128
    z = contract(proj_ref[...], feats_ref[...], (0, 1))
    inverse = 1.0 / jnp.sqrt(jnp.sum(z * z, axis=0, keepdims=True) + epsilon)
    scaled = z * inverse
    unit_ref[...] = scaled
    queries = scaled.astype(bf16)
    query_ref[...] = queries
    plain_ref[...] = queries.T
    count = queries.shape[1]
    positives = positives_ref[...]
    tail = message_ref[rows : rows + tail_rows, :]
    own = []
    pos_id = jnp.zeros((1, count), f32)
    for half in range(halves):
        spot = lax.broadcasted_iota(jnp.int32, (128, count), 0) + half * 128
        own.append(spot == positives)
        found = jnp.dot(tail, own[half].astype(f32).astype(bf16), preferred_element_type=f32)
        for step, scale in enumerate((65536.0, 256.0, 1.0)):
            line = step * halves + half
            pos_id = pos_id + scale * found[line : line + 1, :]
    table = column_table(halves)
    table_ref[...] = table
    own = jnp.concatenate(own, axis=0)
    items = message_ref[0:rows, :]
    ids, logs = item_columns(message_ref, table)
    scores = jnp.dot(items, queries, preferred_element_type=f32)
    scores = scores * (inverse_softness * log2e) - wide(logs, count)
    collide = (wide(ids, count) == pos_id) & jnp.logical_not(own)
    weights = jnp.where(collide, 0.0, jnp.exp2(scores))
    weights_ref[...] = weights
    totals = jnp.sum(weights, axis=0, keepdims=True)
    target = jnp.sum(jnp.where(own, scores, 0.0), axis=0, keepdims=True)
    weighted = contract(items, weights.astype(bf16), (0, 0))
    pos_items = contract(items, own.astype(f32).astype(bf16), (0, 0))
    weighted_ref[...] = weighted
    pos_ref[...] = pos_items
    lines_ref[...] = jnp.concatenate([totals, target * ln2, pos_id, inverse, jnp.zeros((4, count), f32)], axis=0)
    turned_ref[...] = feats_ref[...].T
    item_turned_ref[...] = item_feats_ref[...].T


def add_block(message_ref, query_ref, lines_ref, table_ref, before_ref, totals, weights_ref, chunk=32):
    rows, count = weights_ref.shape
    pos_id = lines_ref[2:3, :]
    partial = jnp.zeros((8, count), f32)
    items = message_ref[0:rows, :]
    ids, logs = item_columns(message_ref, table_ref[...])
    scores = jnp.dot(items, query_ref[...], preferred_element_type=f32)
    rounded = []
    for first in range(0, rows, chunk):
        part = slice(first, first + chunk)
        exponent = scores[part] * (inverse_softness * log2e) - wide(logs[part], count)
        weights = jnp.where(wide(ids[part], count) == pos_id, 0.0, jnp.exp2(exponent))
        for line in range(0, chunk, 8):
            partial = partial + weights[line : line + 8]
        rounded.append(weights.astype(bf16))
    rounded = jnp.concatenate(rounded, axis=0)
    weights_ref[...] = rounded
    weighted = before_ref[...] + contract(items, rounded, (0, 0))
    return totals + jnp.sum(partial, axis=0, keepdims=True), weighted


def middle_block(message_ref, query_ref, lines_ref, table_ref, before_ref, totals_ref, weights_ref, after_ref, sums_ref):
    totals, weighted = add_block(message_ref, query_ref, lines_ref, table_ref, before_ref, totals_ref[0:1, :], weights_ref)
    after_ref[...] = weighted
    sums_ref[...] = jnp.broadcast_to(totals, sums_ref.shape)


def last_block(scale, others, chain, *refs):
    (
        message_ref,
        query_ref,
        lines_ref,
        table_ref,
        before_ref,
        totals_ref,
        pos_ref,
        unit_ref,
        turned_ref,
    ) = refs[:9]
    weights_refs = refs[9 : 8 + others]
    piece_refs = refs[8 + others : 8 + 2 * others]
    own_grad_ref, sums_ref, last_ref, grad_ref = refs[8 + 2 * others :]
    rows, count = last_ref.shape
    totals, weighted = add_block(message_ref, query_ref, lines_ref, table_ref, before_ref, totals_ref[0:1, :], last_ref)
    share = 1.0 / totals
    sums_ref[...] = jnp.concatenate([totals, share, jnp.zeros((6, count), f32)], axis=0)
    cot = weighted * share - pos_ref[...]
    unit = unit_ref[...]
    along = jnp.sum(unit * cot, axis=0, keepdims=True)
    dz = ((cot - unit * along) * (lines_ref[3:4, :] * scale)).astype(bf16)
    shared = (query_ref[...].astype(f32) * share).astype(bf16)
    for step, weights_ref in zip(chain, list(weights_refs) + [last_ref]):
        piece_refs[step - 1][0:rows, :] = contract(weights_ref[...], shared, (1, 1)).astype(bf16)
    grad_ref[...] = contract(turned_ref[...], dz, (1, 1))
    part = grad_ref.shape[0] // 2
    side = lax.rem(lax.axis_index("neg"), 2)
    own_grad_ref[...] = grad_ref[pl.ds(pl.multiple_of(side * part, part), part), :]
    sent = grad_ref[pl.ds(pl.multiple_of((1 - side) * part, part), part), :]
    piece_refs[0][rows : rows + part, :] = sent.astype(bf16)


def own_block(sums_ref, lines_ref, positives_ref, weights_ref, plain_ref, own_ref, losses_ref):
    losses_ref[...] = jnp.log(sums_ref[0:1, :]) - lines_ref[1:2, :]
    own = lax.broadcasted_iota(jnp.int32, weights_ref.shape, 0) == positives_ref[...]
    grads = (weights_ref[...] * sums_ref[1:2, :] - own.astype(f32)).astype(bf16)
    own_ref[...] = jnp.dot(grads, plain_ref[...], preferred_element_type=f32)


def item_gradient(scale, others, own_ref, own_grad_ref, unit_ref, inverse_ref, turned_ref, *refs):
    keep_ref, send_ref = refs[others:]
    rows = own_ref.shape[0]
    cot = own_ref[...]
    query_grad = own_grad_ref[...]
    for ref in refs[:others]:
        cot = cot + ref[0:rows, :].astype(f32)
        if ref.shape[0] > rows:
            query_grad = query_grad + ref[rows:, :].astype(f32)
    unit = unit_ref[...]
    along = jnp.sum(unit * cot, axis=1, keepdims=True)
    dz = ((cot - unit * along) * (inverse_ref[...] * scale)).astype(bf16)
    grad = jnp.dot(turned_ref[...], dz, preferred_element_type=f32)
    first = lax.axis_index("sub") == 0
    for start, whole in ((0, grad), (grad.shape[0] // 2, query_grad)):
        half = whole.shape[0] // 2
        keep_ref[start : start + half, :] = jnp.where(first, whole[:half], whole[half:])
        send_ref[start : start + half, :] = jnp.where(first, whole[half:], whole[:half]).astype(bf16)


def add_pieces(turns, item_rows, own_ref, *refs):
    out_ref = refs[-1]
    values = [own_ref[...].astype(f32)]
    for step in range(1, len(turns) + 1):
        values.append(refs[turns.index(step)][...].astype(f32))
    sums = [values[0], values[1]]
    if len(values) == 4:
        sums = [values[0] + values[2], values[1] + values[3]]
    out_ref[0:item_rows, :] = (sums[0] + sums[1])[:item_rows].astype(bf16)
    query_rows = own_ref.shape[0] - item_rows
    for step, value in enumerate(sums):
        start = item_rows + step * query_rows
        out_ref[start : start + query_rows, :] = value[item_rows:].astype(bf16)


def place_kernel(direct, other, *refs):
    values_ref = refs[0]
    query_hbm, item_hbm, wide_ref, sems = refs[-4:]
    sub = lax.axis_index("sub")
    side = 1 - sub if other else sub
    base = lax.rem(lax.axis_index("neg"), 2) if direct else 0
    half = item_hbm.shape[0] // 2
    part = half // 2
    wide_ref[...] = values_ref[...].astype(f32)
    copies = [
        pltpu.make_async_copy(
            wide_ref.at[pl.ds(0, half)], item_hbm.at[pl.ds(pl.multiple_of(side * half, half), half)], sems.at[2]
        )
    ]
    for step in range(2):
        start = pl.multiple_of((base ^ step) * half + side * part, part)
        copies.append(
            pltpu.make_async_copy(
                wide_ref.at[pl.ds(half + step * part, part)], query_hbm.at[pl.ds(start, part)], sems.at[step]
            )
        )
    for copy in copies:
        copy.start()
    for copy in copies:
        copy.wait()


def place(direct, other, values, outs):
    hbm = pl.BlockSpec(memory_space=pltpu.HBM)
    shape = jax.ShapeDtypeStruct(values.shape, f32)
    return pl.pallas_call(
        functools.partial(place_kernel, direct, other),
        out_shape=(shape, shape),
        in_specs=[pl.BlockSpec(memory_space=pltpu.VMEM)] + [hbm] * len(outs),
        out_specs=(hbm, hbm),
        input_output_aliases={1: 0, 2: 1} if outs else {},
        scratch_shapes=[pltpu.VMEM(values.shape, f32), pltpu.SemaphoreType.DMA((3,))],
        compiler_params=pltpu.CompilerParams(vmem_limit_bytes=32 * 1024 * 1024),
        cost_estimate=pl.CostEstimate(flops=0, bytes_accessed=6 * values.size, transcendentals=0),
    )(values, *outs)


def call(kernel, outs, args, scratch=(), flops=0, fetch=False, room=32):
    vmem = pl.BlockSpec(memory_space=pltpu.VMEM)
    moved = sum(math.prod(s.shape) * s.dtype.itemsize for s in list(outs) + list(args))
    return pl.pallas_call(
        kernel,
        out_shape=tuple(jax.ShapeDtypeStruct(s.shape, s.dtype) for s in outs),
        in_specs=[pl.BlockSpec(memory_space=pltpu.HBM) if fetch else vmem] * len(args),
        out_specs=tuple([vmem] * len(outs)),
        scratch_shapes=list(scratch),
        compiler_params=pltpu.CompilerParams(vmem_limit_bytes=room * 1024 * 1024),
        cost_estimate=pl.CostEstimate(flops=flops, bytes_accessed=moved, transcendentals=0),
    )(*args)


def pin(values):
    return pltpu.with_memory_space_constraint(values, pltpu.HBM)


def out(shape, dtype=f32):
    return jax.ShapeDtypeStruct(shape, dtype)


def partner_of(me, step, count):
    if count & (count - 1) == 0:
        return me ^ step
    return lax.rem(me + step, count)


def source_of(me, step, count):
    return partner_of(me, step if count & (count - 1) == 0 else count - step, count)


def partners(count):
    return [[(j, int(partner_of(j, step, count))) for j in range(count)] for step in range(1, count)]


def ordered(others, order):
    return list(order) if len(order) == others else list(range(1, others + 1))


def sent_back(pairs):
    return [(target, source) for source, target in pairs]


def sum_over(values, axis):
    size = lax.axis_size(axis)
    if size == 1:
        return values
    if size not in (2, 4):
        return lax.psum(values, axis)
    values = values.astype(bf16)
    got = [lax.ppermute(values, axis, pairs).astype(f32) for pairs in partners(size)]
    total = values.astype(f32) + got[0]
    return total + (got[1] + got[2]) if size == 4 else total


def on_device(query_feats, item_feats, query_proj, item_proj, item_ids, item_counts, positives):
    count, hidden = query_feats.shape
    rows = item_feats.shape[0]
    width = query_proj.shape[1]
    scale = inverse_softness / count
    halves = rows // 128
    ring = lax.axis_size("neg")
    exchange = partners(ring)
    others = len(exchange)
    part = hidden // 2
    message, item_unit, item_inverse, query_feats, query_proj, spots, item_feats = call(
        item_tower,
        [
            out((rows + tail_rows, width), bf16),
            out((rows, width)),
            out((rows, width)),
            out((count, hidden), bf16),
            out((hidden, width), bf16),
            out((1, count), jnp.int32),
            out((rows, hidden), bf16),
        ],
        [
            pin(query_feats),
            pin(query_proj),
            pin(positives.reshape(1, count)),
            pin(item_ids.reshape(halves, 128)),
            pin(item_counts.reshape(halves, 128)),
            pin(item_feats),
            pin(item_proj),
        ],
        scratch=[
            pltpu.VMEM((halves, 128), jnp.int32),
            pltpu.VMEM((halves, 128), jnp.int32),
            pltpu.VMEM((hidden, width), bf16),
            pltpu.SemaphoreType.DMA((7,)),
        ],
        flops=2 * rows * hidden * width,
        fetch=True,
        room=32,
    )
    received = [lax.ppermute(message, "neg", pairs) for pairs in exchange]
    query_unit, queries, plain, own_weights, weighted, pos_items, lines, turned, item_turned, table = call(
        query_tower,
        [
            out((width, count)),
            out((width, count), bf16),
            out((count, width), bf16),
            out((rows, count)),
            out((width, count)),
            out((width, count)),
            out((8, count)),
            out((hidden, count), bf16),
            out((hidden, rows), bf16),
            out((tail_rows, 2 * rows), bf16),
        ],
        [query_feats, query_proj, message, spots, item_feats],
        flops=2 * count * width * (hidden + 3 * rows),
    )
    totals = lines
    weights = []
    chain = ordered(others, (3, 1, 2))
    for step in chain[:-1]:
        block = received[step - 1]
        block_weights, weighted, totals = call(
            middle_block,
            [out((rows, count), bf16), out((width, count)), out((8, count))],
            [block, queries, lines, table, weighted, totals],
            flops=4 * count * width * rows,
        )
        weights.append(block_weights)
    results = call(
        functools.partial(last_block, scale, others, chain),
        [out((rows + part, width), bf16)] + [out((rows, width), bf16)] * (others - 1) + [out((part, width)), out((8, count))],
        [received[chain[-1] - 1], queries, lines, table, weighted, totals, pos_items, query_unit, turned] + weights,
        scratch=[pltpu.VMEM((rows, count), bf16), pltpu.VMEM((hidden, width), f32)],
        flops=6 * count * width * rows * (others + 1),
    )
    own_grad, sums = results[others:]
    back = [lax.ppermute(piece, "neg", sent_back(pairs)) for piece, pairs in zip(results, exchange)]
    own_piece, losses = call(
        own_block,
        [out((rows, width)), out((1, count))],
        [sums, lines, spots, own_weights, plain],
        flops=2 * rows * width * count,
    )
    kept = (hidden + part) // 2
    keep, send = call(
        functools.partial(item_gradient, scale, others),
        [out((kept, width)), out((kept, width), bf16)],
        [own_piece, own_grad, item_unit, item_inverse, item_turned] + [back[step - 1] for step in ordered(others, (1, 3, 2))],
        flops=2 * rows * width * hidden,
    )
    swap = [(0, 1), (1, 0)]
    half = sum_over(keep + lax.ppermute(send, "sub", swap).astype(f32), "rep")
    direct = ring in (2, 4)
    if direct:
        half = half.astype(bf16)
        got = [lax.ppermute(half, "neg", pairs) for pairs in exchange]
        turns = ordered(others, (1, 3, 2))
        mine = call(
            functools.partial(add_pieces, turns, hidden // 2),
            [out((hidden, width), bf16)],
            [half] + [got[step - 1] for step in turns],
        )[0]
    else:
        item_half, query_half = half[: hidden // 2], half[hidden // 2 :]
        first = lax.rem(lax.axis_index("neg"), 2) == 0
        none = jnp.zeros_like(query_half)
        both = [item_half, jnp.where(first, query_half, none), jnp.where(first, none, query_half)]
        mine = lax.psum(jnp.concatenate(both, axis=0), "neg").astype(bf16)
    other = lax.ppermute(mine, "sub", swap)
    outs = place(direct, False, mine, ())
    grad_query, grad_item = place(direct, True, other, outs)
    return (grad_query, grad_item, losses.reshape(count))


def solution(mesh):
    split = ("groups", "neg", "rep", "sub")
    return jax.shard_map(
        on_device,
        mesh=mesh,
        in_specs=(P(split, None), P(split, None), P(), P(), P(split), P(split), P(split)),
        out_specs=(P("groups", None), P("groups", None), P(split)),
        check_vma=False,
    )
```

```python
import functools
import math

import jax
import jax.numpy as jnp
from jax import lax
from jax.experimental import pallas as pl
from jax.experimental.pallas import tpu as pltpu
from jax.sharding import PartitionSpec as P

inverse_softness = 20.0
epsilon = 1e-06
log2e = math.log2(math.e)
ln2 = math.log(2.0)
tail_rows = 16
f32 = jnp.float32
bf16 = jnp.bfloat16


def contract(lhs, rhs, over):
    return lax.dot_general(lhs, rhs, (((over[0],), (over[1],)), ((), ())), preferred_element_type=f32)


def split_terms(values):
    terms = []
    for _ in range(3):
        term = values.astype(bf16).astype(f32)
        terms.append(term)
        values = values - term
    return terms


def item_tower(*refs):
    hbm, rest = refs[:7], refs[7:]
    message_ref, unit_ref, inverse_ref = rest[:3]
    targets = rest[3:6] + rest[7:9] + rest[6:7] + rest[9:10]
    sems = rest[10]
    copies = [pltpu.make_async_copy(source, target, sems.at[k]) for k, (source, target) in enumerate(zip(hbm, targets))]
    order = (5, 6, 3, 4, 0, 1, 2)
    for k in order:
        copies[k].start()
    feats_ref, proj_ref, ids_ref, counts_ref = targets[5], targets[6], targets[3], targets[4]
    rows = feats_ref.shape[0]
    copies[3].wait()
    copies[4].wait()
    ids = ids_ref[...]
    digits = [ids >> 16, (ids >> 8) & 255, ids & 255]
    log_counts = jnp.log(counts_ref[...].astype(f32)) * log2e
    lines = [digit.astype(f32) for digit in digits] + split_terms(log_counts)
    halves = ids.shape[0]
    lines.append(jnp.zeros((tail_rows - 6 * halves, ids.shape[1]), f32))
    message_ref[rows : rows + tail_rows, :] = jnp.concatenate(lines, axis=0).astype(bf16)
    copies[6].wait()
    copies[5].wait()
    z = jnp.dot(feats_ref[...], proj_ref[...], preferred_element_type=f32)
    inverse = 1.0 / jnp.sqrt(jnp.sum(z * z, axis=1, keepdims=True) + epsilon)
    unit = z * inverse
    message_ref[0:rows, :] = unit.astype(bf16)
    unit_ref[...] = unit
    inverse_ref[...] = jnp.broadcast_to(inverse, inverse_ref.shape)
    for k in (0, 1, 2):
        copies[k].wait()


def column_table(halves):
    line = lax.broadcasted_iota(jnp.int32, (tail_rows, 128), 0)
    parts = []
    for first, scales in ((0, (65536.0, 256.0, 1.0)), (3, (1.0, 1.0, 1.0))):
        for half in range(halves):
            part = jnp.zeros((tail_rows, 128), f32)
            for step, scale in enumerate(scales):
                part = jnp.where(line == (first + step) * halves + half, scale, part)
            parts.append(part)
    return jnp.concatenate(parts, axis=1).astype(bf16)


def item_columns(message_ref, table):
    rows = message_ref.shape[0] - tail_rows
    halves = rows // 128
    columns = contract(message_ref[rows : rows + tail_rows, :], table, (0, 0))
    ids = [columns[:, half * 128 : half * 128 + 128] for half in range(halves)]
    logs = [columns[:, (halves + half) * 128 : (halves + half) * 128 + 128] for half in range(halves)]
    return jnp.concatenate(ids, axis=0), jnp.concatenate(logs, axis=0)


def wide(column, width):
    return jnp.concatenate([column] * (width // column.shape[1]), axis=1)


def query_tower(
    feats_ref,
    proj_ref,
    message_ref,
    positives_ref,
    item_feats_ref,
    unit_ref,
    query_ref,
    plain_ref,
    weights_ref,
    weighted_ref,
    pos_ref,
    lines_ref,
    turned_ref,
    item_turned_ref,
    table_ref,
):
    rows = message_ref.shape[0] - tail_rows
    halves = rows // 128
    z = contract(proj_ref[...], feats_ref[...], (0, 1))
    inverse = 1.0 / jnp.sqrt(jnp.sum(z * z, axis=0, keepdims=True) + epsilon)
    scaled = z * inverse
    unit_ref[...] = scaled
    queries = scaled.astype(bf16)
    query_ref[...] = queries
    plain_ref[...] = queries.T
    count = queries.shape[1]
    positives = positives_ref[...]
    tail = message_ref[rows : rows + tail_rows, :]
    own = []
    pos_id = jnp.zeros((1, count), f32)
    for half in range(halves):
        spot = lax.broadcasted_iota(jnp.int32, (128, count), 0) + half * 128
        own.append(spot == positives)
        found = jnp.dot(tail, own[half].astype(f32).astype(bf16), preferred_element_type=f32)
        for step, scale in enumerate((65536.0, 256.0, 1.0)):
            line = step * halves + half
            pos_id = pos_id + scale * found[line : line + 1, :]
    table = column_table(halves)
    table_ref[...] = table
    own = jnp.concatenate(own, axis=0)
    items = message_ref[0:rows, :]
    ids, logs = item_columns(message_ref, table)
    scores = jnp.dot(items, queries, preferred_element_type=f32)
    scores = scores * (inverse_softness * log2e) - wide(logs, count)
    collide = (wide(ids, count) == pos_id) & jnp.logical_not(own)
    weights = jnp.where(collide, 0.0, jnp.exp2(scores))
    weights_ref[...] = weights
    totals = jnp.sum(weights, axis=0, keepdims=True)
    target = jnp.sum(jnp.where(own, scores, 0.0), axis=0, keepdims=True)
    weighted = contract(items, weights.astype(bf16), (0, 0))
    pos_items = contract(items, own.astype(f32).astype(bf16), (0, 0))
    weighted_ref[...] = weighted
    pos_ref[...] = pos_items
    lines_ref[...] = jnp.concatenate([totals, target * ln2, pos_id, inverse, jnp.zeros((4, count), f32)], axis=0)
    turned_ref[...] = feats_ref[...].T
    item_turned_ref[...] = item_feats_ref[...].T


def add_block(message_ref, query_ref, lines_ref, table_ref, before_ref, totals, weights_ref, chunk=32):
    rows, count = weights_ref.shape
    pos_id = lines_ref[2:3, :]
    partial = jnp.zeros((8, count), f32)
    items = message_ref[0:rows, :]
    ids, logs = item_columns(message_ref, table_ref[...])
    scores = jnp.dot(items, query_ref[...], preferred_element_type=f32)
    rounded = []
    for first in range(0, rows, chunk):
        part = slice(first, first + chunk)
        exponent = scores[part] * (inverse_softness * log2e) - wide(logs[part], count)
        weights = jnp.where(wide(ids[part], count) == pos_id, 0.0, jnp.exp2(exponent))
        for line in range(0, chunk, 8):
            partial = partial + weights[line : line + 8]
        rounded.append(weights.astype(bf16))
    rounded = jnp.concatenate(rounded, axis=0)
    weights_ref[...] = rounded
    weighted = before_ref[...] + contract(items, rounded, (0, 0))
    return totals + jnp.sum(partial, axis=0, keepdims=True), weighted


def middle_block(message_ref, query_ref, lines_ref, table_ref, before_ref, totals_ref, weights_ref, after_ref, sums_ref):
    totals, weighted = add_block(message_ref, query_ref, lines_ref, table_ref, before_ref, totals_ref[0:1, :], weights_ref)
    after_ref[...] = weighted
    sums_ref[...] = jnp.broadcast_to(totals, sums_ref.shape)


def last_block(scale, others, chain, *refs):
    (
        message_ref,
        query_ref,
        lines_ref,
        table_ref,
        before_ref,
        totals_ref,
        pos_ref,
        unit_ref,
        turned_ref,
    ) = refs[:9]
    weights_refs = refs[9 : 8 + others]
    piece_refs = refs[8 + others : 8 + 2 * others]
    dz_ref, sums_ref, last_ref = refs[8 + 2 * others :]
    rows, count = last_ref.shape
    totals, weighted = add_block(message_ref, query_ref, lines_ref, table_ref, before_ref, totals_ref[0:1, :], last_ref)
    share = 1.0 / totals
    sums_ref[...] = jnp.concatenate([totals, share, jnp.zeros((6, count), f32)], axis=0)
    cot = weighted * share - pos_ref[...]
    unit = unit_ref[...]
    along = jnp.sum(unit * cot, axis=0, keepdims=True)
    dz = ((cot - unit * along) * (lines_ref[3:4, :] * scale)).astype(bf16)
    shared = (query_ref[...].astype(f32) * share).astype(bf16)
    for step, weights_ref in zip(chain, list(weights_refs) + [last_ref]):
        piece_refs[step - 1][0:rows, :] = contract(weights_ref[...], shared, (1, 1)).astype(bf16)
    part = turned_ref.shape[0] // 2
    side = lax.rem(lax.axis_index("neg"), 2)
    dz_ref[...] = dz
    other = turned_ref[pl.ds(pl.multiple_of((1 - side) * part, part), part), :]
    piece_refs[0][rows : rows + part, :] = contract(other, dz, (1, 1)).astype(bf16)


def own_block(
    sums_ref, lines_ref, positives_ref, weights_ref, plain_ref, turned_ref, dz_ref, own_ref, losses_ref, own_grad_ref
):
    part = own_grad_ref.shape[0]
    side = lax.rem(lax.axis_index("neg"), 2)
    mine = turned_ref[pl.ds(pl.multiple_of(side * part, part), part), :]
    own_grad_ref[...] = contract(mine, dz_ref[...], (1, 1))
    losses_ref[...] = jnp.log(sums_ref[0:1, :]) - lines_ref[1:2, :]
    own = lax.broadcasted_iota(jnp.int32, weights_ref.shape, 0) == positives_ref[...]
    grads = (weights_ref[...] * sums_ref[1:2, :] - own.astype(f32)).astype(bf16)
    own_ref[...] = jnp.dot(grads, plain_ref[...], preferred_element_type=f32)


def item_gradient(scale, others, own_ref, own_grad_ref, unit_ref, inverse_ref, turned_ref, *refs):
    keep_ref, send_ref = refs[others:]
    rows = own_ref.shape[0]
    cot = own_ref[...]
    query_grad = own_grad_ref[...]
    for ref in refs[:others]:
        cot = cot + ref[0:rows, :].astype(f32)
        if ref.shape[0] > rows:
            query_grad = query_grad + ref[rows:, :].astype(f32)
    unit = unit_ref[...]
    along = jnp.sum(unit * cot, axis=1, keepdims=True)
    dz = ((cot - unit * along) * (inverse_ref[...] * scale)).astype(bf16)
    grad = jnp.dot(turned_ref[...], dz, preferred_element_type=f32)
    first = lax.axis_index("sub") == 0
    for start, whole in ((0, grad), (grad.shape[0] // 2, query_grad)):
        half = whole.shape[0] // 2
        keep_ref[start : start + half, :] = jnp.where(first, whole[:half], whole[half:])
        send_ref[start : start + half, :] = jnp.where(first, whole[half:], whole[:half]).astype(bf16)


def add_pieces(turns, item_rows, own_ref, *refs):
    out_ref = refs[-1]
    values = [own_ref[...].astype(f32)]
    for step in range(1, len(turns) + 1):
        values.append(refs[turns.index(step)][...].astype(f32))
    sums = [values[0], values[1]]
    if len(values) == 4:
        sums = [values[0] + values[2], values[1] + values[3]]
    out_ref[0:item_rows, :] = (sums[0] + sums[1])[:item_rows].astype(bf16)
    query_rows = own_ref.shape[0] - item_rows
    for step, value in enumerate(sums):
        start = item_rows + step * query_rows
        out_ref[start : start + query_rows, :] = value[item_rows:].astype(bf16)


def place_kernel(direct, other, *refs):
    values_ref = refs[0]
    query_hbm, item_hbm, wide_ref, sems = refs[-4:]
    sub = lax.axis_index("sub")
    side = 1 - sub if other else sub
    base = lax.rem(lax.axis_index("neg"), 2) if direct else 0
    half = item_hbm.shape[0] // 2
    part = half // 2
    wide_ref[...] = values_ref[...].astype(f32)
    copies = [
        pltpu.make_async_copy(
            wide_ref.at[pl.ds(0, half)], item_hbm.at[pl.ds(pl.multiple_of(side * half, half), half)], sems.at[2]
        )
    ]
    for step in range(2):
        start = pl.multiple_of((base ^ step) * half + side * part, part)
        copies.append(
            pltpu.make_async_copy(
                wide_ref.at[pl.ds(half + step * part, part)], query_hbm.at[pl.ds(start, part)], sems.at[step]
            )
        )
    for copy in copies:
        copy.start()
    for copy in copies:
        copy.wait()


def place(direct, other, values, outs):
    hbm = pl.BlockSpec(memory_space=pltpu.HBM)
    shape = jax.ShapeDtypeStruct(values.shape, f32)
    return pl.pallas_call(
        functools.partial(place_kernel, direct, other),
        out_shape=(shape, shape),
        in_specs=[pl.BlockSpec(memory_space=pltpu.VMEM)] + [hbm] * len(outs),
        out_specs=(hbm, hbm),
        input_output_aliases={1: 0, 2: 1} if outs else {},
        scratch_shapes=[pltpu.VMEM(values.shape, f32), pltpu.SemaphoreType.DMA((3,))],
        compiler_params=pltpu.CompilerParams(vmem_limit_bytes=32 * 1024 * 1024),
        cost_estimate=pl.CostEstimate(flops=0, bytes_accessed=6 * values.size, transcendentals=0),
    )(values, *outs)


def call(kernel, outs, args, scratch=(), flops=0, fetch=False, room=32):
    vmem = pl.BlockSpec(memory_space=pltpu.VMEM)
    moved = sum(math.prod(s.shape) * s.dtype.itemsize for s in list(outs) + list(args))
    return pl.pallas_call(
        kernel,
        out_shape=tuple(jax.ShapeDtypeStruct(s.shape, s.dtype) for s in outs),
        in_specs=[pl.BlockSpec(memory_space=pltpu.HBM) if fetch else vmem] * len(args),
        out_specs=tuple([vmem] * len(outs)),
        scratch_shapes=list(scratch),
        compiler_params=pltpu.CompilerParams(vmem_limit_bytes=room * 1024 * 1024),
        cost_estimate=pl.CostEstimate(flops=flops, bytes_accessed=moved, transcendentals=0),
    )(*args)


def pin(values):
    return pltpu.with_memory_space_constraint(values, pltpu.HBM)


def out(shape, dtype=f32):
    return jax.ShapeDtypeStruct(shape, dtype)


def partner_of(me, step, count):
    if count & (count - 1) == 0:
        return me ^ step
    return lax.rem(me + step, count)


def source_of(me, step, count):
    return partner_of(me, step if count & (count - 1) == 0 else count - step, count)


def partners(count):
    return [[(j, int(partner_of(j, step, count))) for j in range(count)] for step in range(1, count)]


def ordered(others, order):
    return list(order) if len(order) == others else list(range(1, others + 1))


def sent_back(pairs):
    return [(target, source) for source, target in pairs]


def sum_over(values, axis):
    size = lax.axis_size(axis)
    if size == 1:
        return values
    if size not in (2, 4):
        return lax.psum(values, axis)
    values = values.astype(bf16)
    got = [lax.ppermute(values, axis, pairs).astype(f32) for pairs in partners(size)]
    total = values.astype(f32) + got[0]
    return total + (got[1] + got[2]) if size == 4 else total


def on_device(query_feats, item_feats, query_proj, item_proj, item_ids, item_counts, positives):
    count, hidden = query_feats.shape
    rows = item_feats.shape[0]
    width = query_proj.shape[1]
    scale = inverse_softness / count
    halves = rows // 128
    ring = lax.axis_size("neg")
    exchange = partners(ring)
    others = len(exchange)
    part = hidden // 2
    message, item_unit, item_inverse, query_feats, query_proj, spots, item_feats = call(
        item_tower,
        [
            out((rows + tail_rows, width), bf16),
            out((rows, width)),
            out((rows, width)),
            out((count, hidden), bf16),
            out((hidden, width), bf16),
            out((1, count), jnp.int32),
            out((rows, hidden), bf16),
        ],
        [
            pin(query_feats),
            pin(query_proj),
            pin(positives.reshape(1, count)),
            pin(item_ids.reshape(halves, 128)),
            pin(item_counts.reshape(halves, 128)),
            pin(item_feats),
            pin(item_proj),
        ],
        scratch=[
            pltpu.VMEM((halves, 128), jnp.int32),
            pltpu.VMEM((halves, 128), jnp.int32),
            pltpu.VMEM((hidden, width), bf16),
            pltpu.SemaphoreType.DMA((7,)),
        ],
        flops=2 * rows * hidden * width,
        fetch=True,
        room=32,
    )
    received = [lax.ppermute(message, "neg", pairs) for pairs in exchange]
    query_unit, queries, plain, own_weights, weighted, pos_items, lines, turned, item_turned, table = call(
        query_tower,
        [
            out((width, count)),
            out((width, count), bf16),
            out((count, width), bf16),
            out((rows, count)),
            out((width, count)),
            out((width, count)),
            out((8, count)),
            out((hidden, count), bf16),
            out((hidden, rows), bf16),
            out((tail_rows, 2 * rows), bf16),
        ],
        [query_feats, query_proj, message, spots, item_feats],
        flops=2 * count * width * (hidden + 3 * rows),
    )
    totals = lines
    weights = []
    chain = ordered(others, (3, 1, 2))
    for step in chain[:-1]:
        block = received[step - 1]
        block_weights, weighted, totals = call(
            middle_block,
            [out((rows, count), bf16), out((width, count)), out((8, count))],
            [block, queries, lines, table, weighted, totals],
            flops=4 * count * width * rows,
        )
        weights.append(block_weights)
    results = call(
        functools.partial(last_block, scale, others, chain),
        [out((rows + part, width), bf16)] + [out((rows, width), bf16)] * (others - 1) + [out((width, count), bf16), out((8, count))],
        [received[chain[-1] - 1], queries, lines, table, weighted, totals, pos_items, query_unit, turned] + weights,
        scratch=[pltpu.VMEM((rows, count), bf16)],
        flops=6 * count * width * rows * (others + 1),
    )
    query_dz, sums = results[others:]
    back = [lax.ppermute(piece, "neg", sent_back(pairs)) for piece, pairs in zip(results, exchange)]
    own_piece, losses, own_grad = call(
        own_block,
        [out((rows, width)), out((1, count)), out((part, width))],
        [sums, lines, spots, own_weights, plain, turned, query_dz],
        flops=2 * (rows + part) * width * count,
    )
    kept = (hidden + part) // 2
    keep, send = call(
        functools.partial(item_gradient, scale, others),
        [out((kept, width)), out((kept, width), bf16)],
        [own_piece, own_grad, item_unit, item_inverse, item_turned] + [back[step - 1] for step in ordered(others, (1, 3, 2))],
        flops=2 * rows * width * hidden,
    )
    swap = [(0, 1), (1, 0)]
    half = sum_over(keep + lax.ppermute(send, "sub", swap).astype(f32), "rep")
    direct = ring in (2, 4)
    if direct:
        half = half.astype(bf16)
        got = [lax.ppermute(half, "neg", pairs) for pairs in exchange]
        turns = ordered(others, (1, 3, 2))
        mine = call(
            functools.partial(add_pieces, turns, hidden // 2),
            [out((hidden, width), bf16)],
            [half] + [got[step - 1] for step in turns],
        )[0]
    else:
        item_half, query_half = half[: hidden // 2], half[hidden // 2 :]
        first = lax.rem(lax.axis_index("neg"), 2) == 0
        none = jnp.zeros_like(query_half)
        both = [item_half, jnp.where(first, query_half, none), jnp.where(first, none, query_half)]
        mine = lax.psum(jnp.concatenate(both, axis=0), "neg").astype(bf16)
    other = lax.ppermute(mine, "sub", swap)
    outs = place(direct, False, mine, ())
    grad_query, grad_item = place(direct, True, other, outs)
    return (grad_query, grad_item, losses.reshape(count))


def solution(mesh):
    split = ("groups", "neg", "rep", "sub")
    return jax.shard_map(
        on_device,
        mesh=mesh,
        in_specs=(P(split, None), P(split, None), P(), P(), P(split), P(split), P(split)),
        out_specs=(P("groups", None), P("groups", None), P(split)),
        check_vma=False,
    )
```

```python
import functools
import math

import jax
import jax.numpy as jnp
from jax import lax
from jax.experimental import pallas as pl
from jax.experimental.pallas import tpu as pltpu
from jax.sharding import PartitionSpec as P

inverse_softness = 20.0
epsilon = 1e-06
log2e = math.log2(math.e)
ln2 = math.log(2.0)
tail_rows = 16
f32 = jnp.float32
bf16 = jnp.bfloat16


def contract(lhs, rhs, over):
    return lax.dot_general(lhs, rhs, (((over[0],), (over[1],)), ((), ())), preferred_element_type=f32)


def split_terms(values):
    terms = []
    for _ in range(3):
        term = values.astype(bf16).astype(f32)
        terms.append(term)
        values = values - term
    return terms


def item_tower(*refs):
    hbm, rest = refs[:7], refs[7:]
    message_ref, unit_ref, inverse_ref = rest[:3]
    targets = rest[3:6] + rest[7:9] + rest[6:7] + rest[9:10]
    sems = rest[10]
    copies = [pltpu.make_async_copy(source, target, sems.at[k]) for k, (source, target) in enumerate(zip(hbm, targets))]
    order = (5, 6, 3, 4, 0, 1, 2)
    for k in order:
        copies[k].start()
    feats_ref, proj_ref, ids_ref, counts_ref = targets[5], targets[6], targets[3], targets[4]
    rows = feats_ref.shape[0]
    copies[3].wait()
    copies[4].wait()
    ids = ids_ref[...]
    digits = [ids >> 16, (ids >> 8) & 255, ids & 255]
    log_counts = jnp.log(counts_ref[...].astype(f32)) * log2e
    lines = [digit.astype(f32) for digit in digits] + split_terms(log_counts)
    halves = ids.shape[0]
    lines.append(jnp.zeros((tail_rows - 6 * halves, ids.shape[1]), f32))
    message_ref[rows : rows + tail_rows, :] = jnp.concatenate(lines, axis=0).astype(bf16)
    copies[6].wait()
    copies[5].wait()
    z = jnp.dot(feats_ref[...], proj_ref[...], preferred_element_type=f32)
    inverse = 1.0 / jnp.sqrt(jnp.sum(z * z, axis=1, keepdims=True) + epsilon)
    unit = z * inverse
    message_ref[0:rows, :] = unit.astype(bf16)
    unit_ref[...] = unit
    inverse_ref[...] = jnp.broadcast_to(inverse, inverse_ref.shape)
    for k in (0, 1, 2):
        copies[k].wait()


def column_table(halves):
    line = lax.broadcasted_iota(jnp.int32, (tail_rows, 128), 0)
    parts = []
    for first, scales in ((0, (65536.0, 256.0, 1.0)), (3, (1.0, 1.0, 1.0))):
        for half in range(halves):
            part = jnp.zeros((tail_rows, 128), f32)
            for step, scale in enumerate(scales):
                part = jnp.where(line == (first + step) * halves + half, scale, part)
            parts.append(part)
    return jnp.concatenate(parts, axis=1).astype(bf16)


def item_columns(message_ref, table):
    rows = message_ref.shape[0] - tail_rows
    halves = rows // 128
    columns = contract(message_ref[rows : rows + tail_rows, :], table, (0, 0))
    ids = [columns[:, half * 128 : half * 128 + 128] for half in range(halves)]
    logs = [columns[:, (halves + half) * 128 : (halves + half) * 128 + 128] for half in range(halves)]
    return jnp.concatenate(ids, axis=0), jnp.concatenate(logs, axis=0)


def wide(column, width):
    return jnp.concatenate([column] * (width // column.shape[1]), axis=1)


def query_tower(
    feats_ref,
    proj_ref,
    message_ref,
    positives_ref,
    item_feats_ref,
    unit_ref,
    query_ref,
    plain_ref,
    weights_ref,
    weighted_ref,
    pos_ref,
    lines_ref,
    turned_ref,
    item_turned_ref,
    table_ref,
):
    rows = message_ref.shape[0] - tail_rows
    halves = rows // 128
    z = contract(proj_ref[...], feats_ref[...], (0, 1))
    inverse = 1.0 / jnp.sqrt(jnp.sum(z * z, axis=0, keepdims=True) + epsilon)
    scaled = z * inverse
    unit_ref[...] = scaled
    queries = scaled.astype(bf16)
    query_ref[...] = queries
    plain_ref[...] = queries.T
    count = queries.shape[1]
    positives = positives_ref[...]
    tail = message_ref[rows : rows + tail_rows, :]
    own = []
    pos_id = jnp.zeros((1, count), f32)
    for half in range(halves):
        spot = lax.broadcasted_iota(jnp.int32, (128, count), 0) + half * 128
        own.append(spot == positives)
        found = jnp.dot(tail, own[half].astype(f32).astype(bf16), preferred_element_type=f32)
        for step, scale in enumerate((65536.0, 256.0, 1.0)):
            line = step * halves + half
            pos_id = pos_id + scale * found[line : line + 1, :]
    table = column_table(halves)
    table_ref[...] = table
    own = jnp.concatenate(own, axis=0)
    items = message_ref[0:rows, :]
    ids, logs = item_columns(message_ref, table)
    scores = jnp.dot(items, queries, preferred_element_type=f32)
    scores = scores * (inverse_softness * log2e) - wide(logs, count)
    collide = (wide(ids, count) == pos_id) & jnp.logical_not(own)
    weights = jnp.where(collide, 0.0, jnp.exp2(scores))
    weights_ref[...] = weights
    totals = jnp.sum(weights, axis=0, keepdims=True)
    target = jnp.sum(jnp.where(own, scores, 0.0), axis=0, keepdims=True)
    weighted = contract(items, weights.astype(bf16), (0, 0))
    pos_items = contract(items, own.astype(f32).astype(bf16), (0, 0))
    weighted_ref[...] = weighted
    pos_ref[...] = pos_items
    lines_ref[...] = jnp.concatenate([totals, target * ln2, pos_id, inverse, jnp.zeros((4, count), f32)], axis=0)
    turned_ref[...] = feats_ref[...].T
    item_turned_ref[...] = item_feats_ref[...].T


def add_block(message_ref, query_ref, lines_ref, table_ref, before_ref, totals, weights_ref, chunk=32):
    rows, count = weights_ref.shape
    pos_id = lines_ref[2:3, :]
    partial = jnp.zeros((8, count), f32)
    items = message_ref[0:rows, :]
    ids, logs = item_columns(message_ref, table_ref[...])
    scores = jnp.dot(items, query_ref[...], preferred_element_type=f32)
    rounded = []
    for first in range(0, rows, chunk):
        part = slice(first, first + chunk)
        exponent = scores[part] * (inverse_softness * log2e) - wide(logs[part], count)
        weights = jnp.where(wide(ids[part], count) == pos_id, 0.0, jnp.exp2(exponent))
        for line in range(0, chunk, 8):
            partial = partial + weights[line : line + 8]
        rounded.append(weights.astype(bf16))
    rounded = jnp.concatenate(rounded, axis=0)
    weights_ref[...] = rounded
    weighted = before_ref[...] + contract(items, rounded, (0, 0))
    return totals + jnp.sum(partial, axis=0, keepdims=True), weighted


def middle_block(message_ref, query_ref, lines_ref, table_ref, before_ref, totals_ref, weights_ref, after_ref, sums_ref):
    totals, weighted = add_block(message_ref, query_ref, lines_ref, table_ref, before_ref, totals_ref[0:1, :], weights_ref)
    after_ref[...] = weighted
    sums_ref[...] = jnp.broadcast_to(totals, sums_ref.shape)


def last_block(scale, others, chain, *refs):
    (
        message_ref,
        query_ref,
        lines_ref,
        table_ref,
        before_ref,
        totals_ref,
        pos_ref,
        unit_ref,
        turned_ref,
    ) = refs[:9]
    weights_refs = refs[9 : 8 + others]
    piece_refs = refs[8 + others : 8 + 2 * others]
    dz_ref, sums_ref, last_ref = refs[8 + 2 * others :]
    rows, count = last_ref.shape
    totals, weighted = add_block(message_ref, query_ref, lines_ref, table_ref, before_ref, totals_ref[0:1, :], last_ref)
    share = 1.0 / totals
    sums_ref[...] = jnp.concatenate([totals, share, jnp.zeros((6, count), f32)], axis=0)
    cot = weighted * share - pos_ref[...]
    unit = unit_ref[...]
    along = jnp.sum(unit * cot, axis=0, keepdims=True)
    dz = ((cot - unit * along) * (lines_ref[3:4, :] * scale)).astype(bf16)
    shared = (query_ref[...].astype(f32) * share).astype(bf16)
    for step, weights_ref in zip(chain, list(weights_refs) + [last_ref]):
        piece_refs[step - 1][0:rows, :] = contract(weights_ref[...], shared, (1, 1)).astype(bf16)
    part = turned_ref.shape[0] // 2
    side = lax.rem(lax.axis_index("neg"), 2)
    dz_ref[...] = dz
    other = turned_ref[pl.ds(pl.multiple_of((1 - side) * part, part), part), :]
    piece_refs[0][rows : rows + part, :] = contract(other, dz, (1, 1)).astype(bf16)


def own_block(
    sums_ref, lines_ref, positives_ref, weights_ref, plain_ref, turned_ref, dz_ref, own_ref, losses_ref, own_grad_ref
):
    part = own_grad_ref.shape[0]
    side = lax.rem(lax.axis_index("neg"), 2)
    mine = turned_ref[pl.ds(pl.multiple_of(side * part, part), part), :]
    own_grad_ref[...] = contract(mine, dz_ref[...], (1, 1))
    losses_ref[...] = jnp.log(sums_ref[0:1, :]) - lines_ref[1:2, :]
    own = lax.broadcasted_iota(jnp.int32, weights_ref.shape, 0) == positives_ref[...]
    grads = (weights_ref[...] * sums_ref[1:2, :] - own.astype(f32)).astype(bf16)
    own_ref[...] = jnp.dot(grads, plain_ref[...], preferred_element_type=f32)


def item_gradient(scale, others, own_ref, own_grad_ref, unit_ref, inverse_ref, turned_ref, *refs):
    keep_ref, send_ref = refs[others:]
    rows = own_ref.shape[0]
    cot = own_ref[...]
    query_grad = own_grad_ref[...]
    for ref in refs[:others]:
        cot = cot + ref[0:rows, :].astype(f32)
        if ref.shape[0] > rows:
            query_grad = query_grad + ref[rows:, :].astype(f32)
    unit = unit_ref[...]
    along = jnp.sum(unit * cot, axis=1, keepdims=True)
    dz = ((cot - unit * along) * (inverse_ref[...] * scale)).astype(bf16)
    grad = jnp.dot(turned_ref[...], dz, preferred_element_type=f32)
    first = lax.axis_index("sub") == 0
    for start, whole in ((0, grad), (grad.shape[0] // 2, query_grad)):
        half = whole.shape[0] // 2
        keep_ref[start : start + half, :] = jnp.where(first, whole[:half], whole[half:])
        send_ref[start : start + half, :] = jnp.where(first, whole[half:], whole[:half]).astype(bf16)


def add_pieces(turns, item_rows, own_ref, *refs):
    out_ref = refs[-1]
    values = [own_ref[...].astype(f32)]
    for step in range(1, len(turns) + 1):
        values.append(refs[turns.index(step)][...].astype(f32))
    sums = [values[0], values[1]]
    if len(values) == 4:
        sums = [values[0] + values[2], values[1] + values[3]]
    out_ref[0:item_rows, :] = (sums[0] + sums[1])[:item_rows].astype(bf16)
    query_rows = own_ref.shape[0] - item_rows
    for step, value in enumerate(sums):
        start = item_rows + step * query_rows
        out_ref[start : start + query_rows, :] = value[item_rows:].astype(bf16)


def place_kernel(direct, other, *refs):
    values_ref = refs[0]
    query_hbm, item_hbm, wide_ref, sems = refs[-4:]
    sub = lax.axis_index("sub")
    side = 1 - sub if other else sub
    base = lax.rem(lax.axis_index("neg"), 2) if direct else 0
    half = item_hbm.shape[0] // 2
    part = half // 2
    wide_ref[...] = values_ref[...].astype(f32)
    copies = [
        pltpu.make_async_copy(
            wide_ref.at[pl.ds(0, half)], item_hbm.at[pl.ds(pl.multiple_of(side * half, half), half)], sems.at[2]
        )
    ]
    for step in range(2):
        start = pl.multiple_of((base ^ step) * half + side * part, part)
        copies.append(
            pltpu.make_async_copy(
                wide_ref.at[pl.ds(half + step * part, part)], query_hbm.at[pl.ds(start, part)], sems.at[step]
            )
        )
    for copy in copies:
        copy.start()
    for copy in copies:
        copy.wait()


def place(direct, other, values, outs):
    hbm = pl.BlockSpec(memory_space=pltpu.HBM)
    shape = jax.ShapeDtypeStruct(values.shape, f32)
    return pl.pallas_call(
        functools.partial(place_kernel, direct, other),
        out_shape=(shape, shape),
        in_specs=[pl.BlockSpec(memory_space=pltpu.VMEM)] + [hbm] * len(outs),
        out_specs=(hbm, hbm),
        input_output_aliases={1: 0, 2: 1} if outs else {},
        scratch_shapes=[pltpu.VMEM(values.shape, f32), pltpu.SemaphoreType.DMA((3,))],
        compiler_params=pltpu.CompilerParams(vmem_limit_bytes=32 * 1024 * 1024),
        cost_estimate=pl.CostEstimate(flops=0, bytes_accessed=6 * values.size, transcendentals=0),
    )(values, *outs)


def call(kernel, outs, args, scratch=(), flops=0, fetch=False, room=32):
    vmem = pl.BlockSpec(memory_space=pltpu.VMEM)
    moved = sum(math.prod(s.shape) * s.dtype.itemsize for s in list(outs) + list(args))
    return pl.pallas_call(
        kernel,
        out_shape=tuple(jax.ShapeDtypeStruct(s.shape, s.dtype) for s in outs),
        in_specs=[pl.BlockSpec(memory_space=pltpu.HBM) if fetch else vmem] * len(args),
        out_specs=tuple([vmem] * len(outs)),
        scratch_shapes=list(scratch),
        compiler_params=pltpu.CompilerParams(vmem_limit_bytes=room * 1024 * 1024),
        cost_estimate=pl.CostEstimate(flops=flops, bytes_accessed=moved, transcendentals=0),
    )(*args)


def pin(values):
    return pltpu.with_memory_space_constraint(values, pltpu.HBM)


def out(shape, dtype=f32):
    return jax.ShapeDtypeStruct(shape, dtype)


def partner_of(me, step, count):
    if count & (count - 1) == 0:
        return me ^ step
    return lax.rem(me + step, count)


def source_of(me, step, count):
    return partner_of(me, step if count & (count - 1) == 0 else count - step, count)


def partners(count):
    return [[(j, int(partner_of(j, step, count))) for j in range(count)] for step in range(1, count)]


def ordered(others, order):
    return list(order) if len(order) == others else list(range(1, others + 1))


def sent_back(pairs):
    return [(target, source) for source, target in pairs]


def sum_over(values, axis):
    size = lax.axis_size(axis)
    if size == 1:
        return values
    if size not in (2, 4):
        return lax.psum(values, axis)
    values = values.astype(bf16)
    got = [lax.ppermute(values, axis, pairs).astype(f32) for pairs in partners(size)]
    total = values.astype(f32) + got[0]
    return total + (got[1] + got[2]) if size == 4 else total


def on_device(query_feats, item_feats, query_proj, item_proj, item_ids, item_counts, positives):
    count, hidden = query_feats.shape
    rows = item_feats.shape[0]
    width = query_proj.shape[1]
    scale = inverse_softness / count
    halves = rows // 128
    ring = lax.axis_size("neg")
    exchange = partners(ring)
    others = len(exchange)
    part = hidden // 2
    message, item_unit, item_inverse, query_feats, query_proj, spots, item_feats = call(
        item_tower,
        [
            out((rows + tail_rows, width), bf16),
            out((rows, width)),
            out((rows, width)),
            out((count, hidden), bf16),
            out((hidden, width), bf16),
            out((1, count), jnp.int32),
            out((rows, hidden), bf16),
        ],
        [
            pin(query_feats),
            pin(query_proj),
            pin(positives.reshape(1, count)),
            pin(item_ids.reshape(halves, 128)),
            pin(item_counts.reshape(halves, 128)),
            pin(item_feats),
            pin(item_proj),
        ],
        scratch=[
            pltpu.VMEM((halves, 128), jnp.int32),
            pltpu.VMEM((halves, 128), jnp.int32),
            pltpu.VMEM((hidden, width), bf16),
            pltpu.SemaphoreType.DMA((7,)),
        ],
        flops=2 * rows * hidden * width,
        fetch=True,
        room=32,
    )
    received = [lax.ppermute(message, "neg", pairs) for pairs in exchange]
    query_unit, queries, plain, own_weights, weighted, pos_items, lines, turned, item_turned, table = call(
        query_tower,
        [
            out((width, count)),
            out((width, count), bf16),
            out((count, width), bf16),
            out((rows, count)),
            out((width, count)),
            out((width, count)),
            out((8, count)),
            out((hidden, count), bf16),
            out((hidden, rows), bf16),
            out((tail_rows, 2 * rows), bf16),
        ],
        [query_feats, query_proj, message, spots, item_feats],
        flops=2 * count * width * (hidden + 3 * rows),
    )
    totals = lines
    weights = []
    chain = ordered(others, (3, 1, 2))
    for step in chain[:-1]:
        block = received[step - 1]
        block_weights, weighted, totals = call(
            middle_block,
            [out((rows, count), bf16), out((width, count)), out((8, count))],
            [block, queries, lines, table, weighted, totals],
            flops=4 * count * width * rows,
        )
        weights.append(block_weights)
    results = call(
        functools.partial(last_block, scale, others, chain),
        [out((rows + part, width), bf16)] + [out((rows, width), bf16)] * (others - 1) + [out((width, count), bf16), out((8, count))],
        [received[chain[-1] - 1], queries, lines, table, weighted, totals, pos_items, query_unit, turned] + weights,
        scratch=[pltpu.VMEM((rows, count), bf16)],
        flops=6 * count * width * rows * (others + 1),
    )
    query_dz, sums = results[others:]
    back = [lax.ppermute(piece, "neg", sent_back(pairs)) for piece, pairs in zip(results, exchange)]
    own_piece, losses, own_grad = call(
        own_block,
        [out((rows, width)), out((1, count)), out((part, width))],
        [sums, lines, spots, own_weights, plain, turned, query_dz],
        flops=2 * (rows + part) * width * count,
    )
    kept = (hidden + part) // 2
    keep, send = call(
        functools.partial(item_gradient, scale, others),
        [out((kept, width)), out((kept, width), bf16)],
        [own_piece, own_grad, item_unit, item_inverse, item_turned] + [back[step - 1] for step in ordered(others, (1, 2, 3))],
        flops=2 * rows * width * hidden,
    )
    swap = [(0, 1), (1, 0)]
    half = sum_over(keep + lax.ppermute(send, "sub", swap).astype(f32), "rep")
    direct = ring in (2, 4)
    if direct:
        half = half.astype(bf16)
        got = [lax.ppermute(half, "neg", pairs) for pairs in exchange]
        turns = ordered(others, (1, 2, 3))
        mine = call(
            functools.partial(add_pieces, turns, hidden // 2),
            [out((hidden, width), bf16)],
            [half] + [got[step - 1] for step in turns],
        )[0]
    else:
        item_half, query_half = half[: hidden // 2], half[hidden // 2 :]
        first = lax.rem(lax.axis_index("neg"), 2) == 0
        none = jnp.zeros_like(query_half)
        both = [item_half, jnp.where(first, query_half, none), jnp.where(first, none, query_half)]
        mine = lax.psum(jnp.concatenate(both, axis=0), "neg").astype(bf16)
    other = lax.ppermute(mine, "sub", swap)
    outs = place(direct, False, mine, ())
    grad_query, grad_item = place(direct, True, other, outs)
    return (grad_query, grad_item, losses.reshape(count))


def solution(mesh):
    split = ("groups", "neg", "rep", "sub")
    return jax.shard_map(
        on_device,
        mesh=mesh,
        in_specs=(P(split, None), P(split, None), P(), P(), P(split), P(split), P(split)),
        out_specs=(P("groups", None), P("groups", None), P(split)),
        check_vma=False,
    )
```

```python
import functools
import math

import jax
import jax.numpy as jnp
from jax import lax
from jax.experimental import pallas as pl
from jax.experimental.pallas import tpu as pltpu
from jax.sharding import PartitionSpec as P

inverse_softness = 20.0
epsilon = 1e-06
log2e = math.log2(math.e)
ln2 = math.log(2.0)
tail_rows = 16
f32 = jnp.float32
bf16 = jnp.bfloat16


def contract(lhs, rhs, over):
    return lax.dot_general(lhs, rhs, (((over[0],), (over[1],)), ((), ())), preferred_element_type=f32)


def split_terms(values):
    terms = []
    for _ in range(3):
        term = values.astype(bf16).astype(f32)
        terms.append(term)
        values = values - term
    return terms


def item_tower(*refs):
    hbm, rest = refs[:7], refs[7:]
    message_ref, unit_ref, inverse_ref = rest[:3]
    targets = rest[3:6] + rest[7:9] + rest[6:7] + rest[9:10]
    sems = rest[10]
    copies = [pltpu.make_async_copy(source, target, sems.at[k]) for k, (source, target) in enumerate(zip(hbm, targets))]
    order = (5, 6, 3, 4, 0, 1, 2)
    for k in order:
        copies[k].start()
    feats_ref, proj_ref, ids_ref, counts_ref = targets[5], targets[6], targets[3], targets[4]
    rows = feats_ref.shape[0]
    copies[3].wait()
    copies[4].wait()
    ids = ids_ref[...]
    digits = [ids >> 16, (ids >> 8) & 255, ids & 255]
    log_counts = jnp.log(counts_ref[...].astype(f32)) * log2e
    lines = [digit.astype(f32) for digit in digits] + split_terms(log_counts)
    halves = ids.shape[0]
    lines.append(jnp.zeros((tail_rows - 6 * halves, ids.shape[1]), f32))
    message_ref[rows : rows + tail_rows, :] = jnp.concatenate(lines, axis=0).astype(bf16)
    copies[6].wait()
    copies[5].wait()
    z = jnp.dot(feats_ref[...], proj_ref[...], preferred_element_type=f32)
    inverse = lax.rsqrt(jnp.sum(z * z, axis=1, keepdims=True) + epsilon)
    unit = z * inverse
    message_ref[0:rows, :] = unit.astype(bf16)
    unit_ref[...] = unit
    inverse_ref[...] = jnp.broadcast_to(inverse, inverse_ref.shape)
    for k in (0, 1, 2):
        copies[k].wait()


def column_table(halves):
    line = lax.broadcasted_iota(jnp.int32, (tail_rows, 128), 0)
    parts = []
    for first, scales in ((0, (65536.0, 256.0, 1.0)), (3, (1.0, 1.0, 1.0))):
        for half in range(halves):
            part = jnp.zeros((tail_rows, 128), f32)
            for step, scale in enumerate(scales):
                part = jnp.where(line == (first + step) * halves + half, scale, part)
            parts.append(part)
    return jnp.concatenate(parts, axis=1).astype(bf16)


def item_columns(message_ref, table):
    rows = message_ref.shape[0] - tail_rows
    halves = rows // 128
    columns = contract(message_ref[rows : rows + tail_rows, :], table, (0, 0))
    ids = [columns[:, half * 128 : half * 128 + 128] for half in range(halves)]
    logs = [columns[:, (halves + half) * 128 : (halves + half) * 128 + 128] for half in range(halves)]
    return jnp.concatenate(ids, axis=0), jnp.concatenate(logs, axis=0)


def wide(column, width):
    return jnp.concatenate([column] * (width // column.shape[1]), axis=1)


def query_tower(
    feats_ref,
    proj_ref,
    message_ref,
    positives_ref,
    item_feats_ref,
    unit_ref,
    query_ref,
    plain_ref,
    weights_ref,
    weighted_ref,
    pos_ref,
    lines_ref,
    turned_ref,
    item_turned_ref,
    table_ref,
):
    rows = message_ref.shape[0] - tail_rows
    halves = rows // 128
    z = contract(proj_ref[...], feats_ref[...], (0, 1))
    inverse = 1.0 / jnp.sqrt(jnp.sum(z * z, axis=0, keepdims=True) + epsilon)
    scaled = z * inverse
    unit_ref[...] = scaled
    queries = scaled.astype(bf16)
    query_ref[...] = queries
    plain_ref[...] = queries.T
    count = queries.shape[1]
    positives = positives_ref[...]
    tail = message_ref[rows : rows + tail_rows, :]
    own = []
    pos_id = jnp.zeros((1, count), f32)
    for half in range(halves):
        spot = lax.broadcasted_iota(jnp.int32, (128, count), 0) + half * 128
        own.append(spot == positives)
        found = jnp.dot(tail, own[half].astype(f32).astype(bf16), preferred_element_type=f32)
        for step, scale in enumerate((65536.0, 256.0, 1.0)):
            line = step * halves + half
            pos_id = pos_id + scale * found[line : line + 1, :]
    table = column_table(halves)
    table_ref[...] = table
    own = jnp.concatenate(own, axis=0)
    items = message_ref[0:rows, :]
    ids, logs = item_columns(message_ref, table)
    scores = jnp.dot(items, queries, preferred_element_type=f32)
    scores = scores * (inverse_softness * log2e) - wide(logs, count)
    collide = (wide(ids, count) == pos_id) & jnp.logical_not(own)
    weights = jnp.where(collide, 0.0, jnp.exp2(scores))
    weights_ref[...] = weights
    totals = jnp.sum(weights, axis=0, keepdims=True)
    target = jnp.sum(jnp.where(own, scores, 0.0), axis=0, keepdims=True)
    weighted = contract(items, weights.astype(bf16), (0, 0))
    pos_items = contract(items, own.astype(f32).astype(bf16), (0, 0))
    weighted_ref[...] = weighted
    pos_ref[...] = pos_items
    lines_ref[...] = jnp.concatenate([totals, target * ln2, pos_id, inverse, jnp.zeros((4, count), f32)], axis=0)
    turned_ref[...] = feats_ref[...].T
    item_turned_ref[...] = item_feats_ref[...].T


def add_block(message_ref, query_ref, lines_ref, table_ref, before_ref, totals, weights_ref, chunk=32):
    rows, count = weights_ref.shape
    pos_id = lines_ref[2:3, :]
    partial = jnp.zeros((8, count), f32)
    items = message_ref[0:rows, :]
    ids, logs = item_columns(message_ref, table_ref[...])
    scores = jnp.dot(items, query_ref[...], preferred_element_type=f32)
    rounded = []
    for first in range(0, rows, chunk):
        part = slice(first, first + chunk)
        exponent = scores[part] * (inverse_softness * log2e) - wide(logs[part], count)
        weights = jnp.where(wide(ids[part], count) == pos_id, 0.0, jnp.exp2(exponent))
        for line in range(0, chunk, 8):
            partial = partial + weights[line : line + 8]
        rounded.append(weights.astype(bf16))
    rounded = jnp.concatenate(rounded, axis=0)
    weights_ref[...] = rounded
    weighted = before_ref[...] + contract(items, rounded, (0, 0))
    return totals + jnp.sum(partial, axis=0, keepdims=True), weighted


def middle_block(message_ref, query_ref, lines_ref, table_ref, before_ref, totals_ref, weights_ref, after_ref, sums_ref):
    totals, weighted = add_block(message_ref, query_ref, lines_ref, table_ref, before_ref, totals_ref[0:1, :], weights_ref)
    after_ref[...] = weighted
    sums_ref[...] = jnp.broadcast_to(totals, sums_ref.shape)


def last_block(scale, others, chain, *refs):
    (
        message_ref,
        query_ref,
        lines_ref,
        table_ref,
        before_ref,
        totals_ref,
        pos_ref,
        unit_ref,
        turned_ref,
    ) = refs[:9]
    weights_refs = refs[9 : 8 + others]
    piece_refs = refs[8 + others : 8 + 2 * others]
    dz_ref, sums_ref, last_ref = refs[8 + 2 * others :]
    rows, count = last_ref.shape
    totals, weighted = add_block(message_ref, query_ref, lines_ref, table_ref, before_ref, totals_ref[0:1, :], last_ref)
    share = 1.0 / totals
    sums_ref[...] = jnp.concatenate([totals, share, jnp.zeros((6, count), f32)], axis=0)
    cot = weighted * share - pos_ref[...]
    unit = unit_ref[...]
    along = jnp.sum(unit * cot, axis=0, keepdims=True)
    dz = ((cot - unit * along) * (lines_ref[3:4, :] * scale)).astype(bf16)
    shared = (query_ref[...].astype(f32) * share).astype(bf16)
    for step, weights_ref in zip(chain, list(weights_refs) + [last_ref]):
        piece_refs[step - 1][0:rows, :] = contract(weights_ref[...], shared, (1, 1)).astype(bf16)
    part = turned_ref.shape[0] // 2
    side = lax.rem(lax.axis_index("neg"), 2)
    dz_ref[...] = dz
    other = turned_ref[pl.ds(pl.multiple_of((1 - side) * part, part), part), :]
    piece_refs[0][rows : rows + part, :] = contract(other, dz, (1, 1)).astype(bf16)


def own_block(
    sums_ref, lines_ref, positives_ref, weights_ref, plain_ref, turned_ref, dz_ref, own_ref, losses_ref, own_grad_ref
):
    part = own_grad_ref.shape[0]
    side = lax.rem(lax.axis_index("neg"), 2)
    mine = turned_ref[pl.ds(pl.multiple_of(side * part, part), part), :]
    own_grad_ref[...] = contract(mine, dz_ref[...], (1, 1))
    losses_ref[...] = jnp.log(sums_ref[0:1, :]) - lines_ref[1:2, :]
    own = lax.broadcasted_iota(jnp.int32, weights_ref.shape, 0) == positives_ref[...]
    grads = (weights_ref[...] * sums_ref[1:2, :] - own.astype(f32)).astype(bf16)
    own_ref[...] = jnp.dot(grads, plain_ref[...], preferred_element_type=f32)


def item_gradient(scale, others, own_ref, own_grad_ref, unit_ref, inverse_ref, turned_ref, *refs):
    keep_ref, send_ref = refs[others:]
    rows = own_ref.shape[0]
    cot = own_ref[...]
    query_grad = own_grad_ref[...]
    for ref in refs[:others]:
        cot = cot + ref[0:rows, :].astype(f32)
        if ref.shape[0] > rows:
            query_grad = query_grad + ref[rows:, :].astype(f32)
    unit = unit_ref[...]
    along = jnp.sum(unit * cot, axis=1, keepdims=True)
    dz = ((cot - unit * along) * (inverse_ref[...] * scale)).astype(bf16)
    grad = jnp.dot(turned_ref[...], dz, preferred_element_type=f32)
    first = lax.axis_index("sub") == 0
    for start, whole in ((0, grad), (grad.shape[0] // 2, query_grad)):
        half = whole.shape[0] // 2
        keep_ref[start : start + half, :] = jnp.where(first, whole[:half], whole[half:])
        send_ref[start : start + half, :] = jnp.where(first, whole[half:], whole[:half]).astype(bf16)


def add_pieces(turns, item_rows, own_ref, *refs):
    out_ref = refs[-1]
    values = [own_ref[...].astype(f32)]
    for step in range(1, len(turns) + 1):
        values.append(refs[turns.index(step)][...].astype(f32))
    sums = [values[0], values[1]]
    if len(values) == 4:
        sums = [values[0] + values[2], values[1] + values[3]]
    out_ref[0:item_rows, :] = (sums[0] + sums[1])[:item_rows].astype(bf16)
    query_rows = own_ref.shape[0] - item_rows
    for step, value in enumerate(sums):
        start = item_rows + step * query_rows
        out_ref[start : start + query_rows, :] = value[item_rows:].astype(bf16)


def place_kernel(direct, other, *refs):
    values_ref = refs[0]
    query_hbm, item_hbm, wide_ref, sems = refs[-4:]
    sub = lax.axis_index("sub")
    side = 1 - sub if other else sub
    base = lax.rem(lax.axis_index("neg"), 2) if direct else 0
    half = item_hbm.shape[0] // 2
    part = half // 2
    wide_ref[...] = values_ref[...].astype(f32)
    copies = [
        pltpu.make_async_copy(
            wide_ref.at[pl.ds(0, half)], item_hbm.at[pl.ds(pl.multiple_of(side * half, half), half)], sems.at[2]
        )
    ]
    for step in range(2):
        start = pl.multiple_of((base ^ step) * half + side * part, part)
        copies.append(
            pltpu.make_async_copy(
                wide_ref.at[pl.ds(half + step * part, part)], query_hbm.at[pl.ds(start, part)], sems.at[step]
            )
        )
    for copy in copies:
        copy.start()
    for copy in copies:
        copy.wait()


def place(direct, other, values, outs):
    hbm = pl.BlockSpec(memory_space=pltpu.HBM)
    shape = jax.ShapeDtypeStruct(values.shape, f32)
    return pl.pallas_call(
        functools.partial(place_kernel, direct, other),
        out_shape=(shape, shape),
        in_specs=[pl.BlockSpec(memory_space=pltpu.VMEM)] + [hbm] * len(outs),
        out_specs=(hbm, hbm),
        input_output_aliases={1: 0, 2: 1} if outs else {},
        scratch_shapes=[pltpu.VMEM(values.shape, f32), pltpu.SemaphoreType.DMA((3,))],
        compiler_params=pltpu.CompilerParams(vmem_limit_bytes=32 * 1024 * 1024),
        cost_estimate=pl.CostEstimate(flops=0, bytes_accessed=6 * values.size, transcendentals=0),
    )(values, *outs)


def call(kernel, outs, args, scratch=(), flops=0, fetch=False, room=32):
    vmem = pl.BlockSpec(memory_space=pltpu.VMEM)
    moved = sum(math.prod(s.shape) * s.dtype.itemsize for s in list(outs) + list(args))
    return pl.pallas_call(
        kernel,
        out_shape=tuple(jax.ShapeDtypeStruct(s.shape, s.dtype) for s in outs),
        in_specs=[pl.BlockSpec(memory_space=pltpu.HBM) if fetch else vmem] * len(args),
        out_specs=tuple([vmem] * len(outs)),
        scratch_shapes=list(scratch),
        compiler_params=pltpu.CompilerParams(vmem_limit_bytes=room * 1024 * 1024),
        cost_estimate=pl.CostEstimate(flops=flops, bytes_accessed=moved, transcendentals=0),
    )(*args)


def pin(values):
    return pltpu.with_memory_space_constraint(values, pltpu.HBM)


def out(shape, dtype=f32):
    return jax.ShapeDtypeStruct(shape, dtype)


def partner_of(me, step, count):
    if count & (count - 1) == 0:
        return me ^ step
    return lax.rem(me + step, count)


def source_of(me, step, count):
    return partner_of(me, step if count & (count - 1) == 0 else count - step, count)


def partners(count):
    return [[(j, int(partner_of(j, step, count))) for j in range(count)] for step in range(1, count)]


def ordered(others, order):
    return list(order) if len(order) == others else list(range(1, others + 1))


def sent_back(pairs):
    return [(target, source) for source, target in pairs]


def sum_over(values, axis):
    size = lax.axis_size(axis)
    if size == 1:
        return values
    if size not in (2, 4):
        return lax.psum(values, axis)
    values = values.astype(bf16)
    got = [lax.ppermute(values, axis, pairs).astype(f32) for pairs in partners(size)]
    total = values.astype(f32) + got[0]
    return total + (got[1] + got[2]) if size == 4 else total


def on_device(query_feats, item_feats, query_proj, item_proj, item_ids, item_counts, positives):
    count, hidden = query_feats.shape
    rows = item_feats.shape[0]
    width = query_proj.shape[1]
    scale = inverse_softness / count
    halves = rows // 128
    ring = lax.axis_size("neg")
    exchange = partners(ring)
    others = len(exchange)
    part = hidden // 2
    message, item_unit, item_inverse, query_feats, query_proj, spots, item_feats = call(
        item_tower,
        [
            out((rows + tail_rows, width), bf16),
            out((rows, width)),
            out((rows, width)),
            out((count, hidden), bf16),
            out((hidden, width), bf16),
            out((1, count), jnp.int32),
            out((rows, hidden), bf16),
        ],
        [
            pin(query_feats),
            pin(query_proj),
            pin(positives.reshape(1, count)),
            pin(item_ids.reshape(halves, 128)),
            pin(item_counts.reshape(halves, 128)),
            pin(item_feats),
            pin(item_proj),
        ],
        scratch=[
            pltpu.VMEM((halves, 128), jnp.int32),
            pltpu.VMEM((halves, 128), jnp.int32),
            pltpu.VMEM((hidden, width), bf16),
            pltpu.SemaphoreType.DMA((7,)),
        ],
        flops=2 * rows * hidden * width,
        fetch=True,
        room=32,
    )
    received = [lax.ppermute(message, "neg", pairs) for pairs in exchange]
    query_unit, queries, plain, own_weights, weighted, pos_items, lines, turned, item_turned, table = call(
        query_tower,
        [
            out((width, count)),
            out((width, count), bf16),
            out((count, width), bf16),
            out((rows, count)),
            out((width, count)),
            out((width, count)),
            out((8, count)),
            out((hidden, count), bf16),
            out((hidden, rows), bf16),
            out((tail_rows, 2 * rows), bf16),
        ],
        [query_feats, query_proj, message, spots, item_feats],
        flops=2 * count * width * (hidden + 3 * rows),
    )
    totals = lines
    weights = []
    chain = ordered(others, (3, 1, 2))
    for step in chain[:-1]:
        block = received[step - 1]
        block_weights, weighted, totals = call(
            middle_block,
            [out((rows, count), bf16), out((width, count)), out((8, count))],
            [block, queries, lines, table, weighted, totals],
            flops=4 * count * width * rows,
        )
        weights.append(block_weights)
    results = call(
        functools.partial(last_block, scale, others, chain),
        [out((rows + part, width), bf16)] + [out((rows, width), bf16)] * (others - 1) + [out((width, count), bf16), out((8, count))],
        [received[chain[-1] - 1], queries, lines, table, weighted, totals, pos_items, query_unit, turned] + weights,
        scratch=[pltpu.VMEM((rows, count), bf16)],
        flops=6 * count * width * rows * (others + 1),
    )
    query_dz, sums = results[others:]
    back = [lax.ppermute(piece, "neg", sent_back(pairs)) for piece, pairs in zip(results, exchange)]
    own_piece, losses, own_grad = call(
        own_block,
        [out((rows, width)), out((1, count)), out((part, width))],
        [sums, lines, spots, own_weights, plain, turned, query_dz],
        flops=2 * (rows + part) * width * count,
    )
    kept = (hidden + part) // 2
    keep, send = call(
        functools.partial(item_gradient, scale, others),
        [out((kept, width)), out((kept, width), bf16)],
        [own_piece, own_grad, item_unit, item_inverse, item_turned] + [back[step - 1] for step in ordered(others, (1, 2, 3))],
        flops=2 * rows * width * hidden,
    )
    swap = [(0, 1), (1, 0)]
    half = sum_over(keep + lax.ppermute(send, "sub", swap).astype(f32), "rep")
    direct = ring in (2, 4)
    if direct:
        half = half.astype(bf16)
        got = [lax.ppermute(half, "neg", pairs) for pairs in exchange]
        turns = ordered(others, (1, 2, 3))
        mine = call(
            functools.partial(add_pieces, turns, hidden // 2),
            [out((hidden, width), bf16)],
            [half] + [got[step - 1] for step in turns],
        )[0]
    else:
        item_half, query_half = half[: hidden // 2], half[hidden // 2 :]
        first = lax.rem(lax.axis_index("neg"), 2) == 0
        none = jnp.zeros_like(query_half)
        both = [item_half, jnp.where(first, query_half, none), jnp.where(first, none, query_half)]
        mine = lax.psum(jnp.concatenate(both, axis=0), "neg").astype(bf16)
    other = lax.ppermute(mine, "sub", swap)
    outs = place(direct, False, mine, ())
    grad_query, grad_item = place(direct, True, other, outs)
    return (grad_query, grad_item, losses.reshape(count))


def solution(mesh):
    split = ("groups", "neg", "rep", "sub")
    return jax.shard_map(
        on_device,
        mesh=mesh,
        in_specs=(P(split, None), P(split, None), P(), P(), P(split), P(split), P(split)),
        out_specs=(P("groups", None), P("groups", None), P(split)),
        check_vma=False,
    )
```
